256 devices in a mesh: gx: 16 (over z, core), yz: 16 (over y, x).
Axes of the slice: x: 4, y: 4, z: 8, core: 2. Of those that a mesh axis runs over, the one named last changes fastest.
Arguments:
- loads: float32 [16, 294912], P(None, ('gx', 'yz')), may hold values from -30 to 30
- stiffness: bfloat16 [294912, 1152], P(('gx', 'yz')), may hold values from -1 to 16, as said below
- local_inverse: bfloat16 [294912, 1152], P(('gx', 'yz')), may hold values from -1 to 2, as said below
- coarse_basis: bfloat16 [24, 294912], P(None, ('gx', 'yz')), may hold values from -0.1875 to 0.1875
- coarse_inverse: bfloat16 [1024, 1024], replicated, may hold values from -1 to 2, as said below
- primal_index: int32 [256, 24], P(('gx', 'yz')), may hold values from 0 to 1023, as said below
- layer_counts: int32 [256, 2], P(('gx', 'yz')), may hold values from 0 to 144, as said below
- layer_index: int32 [256, 2, 144], P(('gx', 'yz')), may hold values from 0 to 1151, as said below
- across_counts: int32 [256, 16], P(('gx', 'yz')), may hold values from 0 to 48, as said below
- across_index: int32 [256, 16, 48], P(('gx', 'yz')), may hold values from 0 to 1151, as said below
Outputs:
- solution: float32 [16, 294912], P(None, ('gx', 'yz'))
- residual: float32 [16, 294912], P(None, ('gx', 'yz'))
- precond: float32 [16, 294912], P(None, ('gx', 'yz'))
The draws below stay inside these ranges and needn't reach their ends.
Inputs may be any that keep to these rules, and one draw needn't show every extreme that they name: `stiffness`: each subdomain's block of 1152 rows is symmetric positive definite. `local_inverse`: each subdomain's block of 1152 rows is symmetric positive definite. `coarse_inverse`: symmetric positive definite. `primal_index`: the 24 entries of one subdomain are distinct. layer_counts[s, 1] equals layer_counts[s + 16, 0]; the lower count is 0 on the first layer and the upper count 0 on the last; for one position p across, drawn afresh, every two adjacent layers share exactly 144 dofs there. `layer_index`: entry j of subdomain s's upper list and entry j of subdomain s + 16's lower list name the same shared dof; entries past a count are 0; all list entries of one subdomain, layer and across lists together, are distinct. across_counts[g * 16 + p, q] equals across_counts[g * 16 + q, p]; it is 0 for q = p, exactly 48 for q = p + 1 and q = p - 1 (mod 16), and in each layer one subdomain shares exactly 48 with every other one. `across_index`: entry j of subdomain s's list toward t and entry j of t's list toward s name the same shared dof; entries past a count are 0.
All inputs are finite; a program needn't handle non-finite values.
Results may differ from the reference program's by a relative error of at most 0.025.
Values may be sent and summed in bfloat16 or wider, within the bound.
A program may use at most 64 MiB of HBM per device.

```python
import math
import jax
import jax.numpy as jnp
from jax import lax

CASES = 16
IFACE = 1152
PRIMAL = 24
ITERS = 2
SLOTS = 48
FACE_SLOTS = 144
LAYERS = 16
ACROSS = 16
SUBDOMAINS = 256
DOFS = 294912
COARSE = 1024


def interface_lists(key):
    keys = jax.random.split(key, 5)
    places = jnp.arange(ACROSS)
    upper = jax.random.randint(keys[0], (LAYERS, ACROSS, ACROSS), 0, SLOTS + 1)
    before = places[:, None] < places[None, :]
    across = jnp.where(before[None], upper, jnp.swapaxes(upper, 1, 2))
    cycle = ((places[None, :] - places[:, None]) % ACROSS == 1) | ((places[:, None] - places[None, :]) % ACROSS == 1)
    center = jax.random.randint(keys[1], (LAYERS, 1, 1), 0, ACROSS)
    busiest = (places[None, :, None] == center) | (places[None, None, :] == center)
    across = jnp.where(cycle[None] | busiest, SLOTS, across)
    across = jnp.where((places[:, None] == places[None, :])[None], 0, across)
    bound = jax.random.randint(keys[2], (LAYERS, ACROSS), FACE_SLOTS // 2, FACE_SLOTS + 1)
    chosen = jax.random.randint(keys[3], (), 0, ACROSS)
    bound = jnp.where(places[None, :] == chosen, FACE_SLOTS, bound)
    layer = jnp.arange(LAYERS)[:, None]
    to_upper = jnp.where(layer < LAYERS - 1, bound, 0)
    to_lower = jnp.where(layer > 0, jnp.roll(bound, 1, axis=0), 0)
    layer_counts = jnp.stack([to_lower, to_upper], -1).reshape(SUBDOMAINS, 2).astype(jnp.int32)
    across_counts = across.reshape(SUBDOMAINS, ACROSS).astype(jnp.int32)
    counts = jnp.concatenate([layer_counts, across_counts], 1)
    starts = jnp.cumsum(counts, 1) - counts
    orders = jax.vmap(lambda sub_key: jax.random.permutation(sub_key, IFACE))(jax.random.split(keys[4], SUBDOMAINS))

    def place(start, count, width):
        slot = jnp.arange(width)
        position = jnp.minimum(start[..., None] + slot, IFACE - 1)
        taken = jax.vmap(lambda ordering, spots: ordering[spots])(orders, position)
        return jnp.where(slot < count[..., None], taken, 0).astype(jnp.int32)
    layer_index = place(starts[:, :2], layer_counts, FACE_SLOTS)
    across_index = place(starts[:, 2:], across_counts, SLOTS)
    return (layer_counts, layer_index, across_counts, across_index)


def draw_layer_counts(key, part):
    return interface_lists(key)[0]


def draw_layer_index(key, part):
    return interface_lists(key)[1]


def draw_across_counts(key, part):
    return interface_lists(key)[2]


def draw_across_index(key, part):
    return interface_lists(key)[3]


def draw_primal_index(key, part):
    key = jax.random.fold_in(key, 7)
    keys = jax.random.split(key, SUBDOMAINS)
    picks = jax.vmap(lambda sub_key: jax.random.permutation(sub_key, COARSE)[:PRIMAL])(keys)
    return picks.astype(jnp.int32)


def symmetric_block(noise, diagonal):
    identity = jnp.eye(diagonal.shape[0], dtype=jnp.float32)
    block = 0.5 * (noise + noise.T) * (1.0 - identity) + identity * diagonal[None, :]
    return block


def draw_stiffness(key, part):
    key = jax.random.fold_in(key, 11)
    keys = jax.random.split(key, SUBDOMAINS)

    def single(sub_key):
        key_diag, key_off = jax.random.split(sub_key, 2)
        diagonal = jnp.exp(jax.random.uniform(key_diag, (IFACE,), minval=math.log(2.0), maxval=math.log(6.0)))
        noise = jax.random.uniform(key_off, (IFACE, IFACE), minval=-1.0, maxval=1.0) * (1.2 / math.sqrt(IFACE))
        return symmetric_block(noise, diagonal).astype(jnp.bfloat16)
    return lax.map(single, keys).reshape(DOFS, IFACE)


def draw_local_inverse(key, part):
    key = jax.random.fold_in(key, 13)
    keys = jax.random.split(key, SUBDOMAINS)

    def single(sub_key):
        key_diag, key_off = jax.random.split(sub_key, 2)
        diagonal = jnp.exp(jax.random.uniform(key_diag, (IFACE,), minval=math.log(0.5), maxval=math.log(1.5)))
        noise = jax.random.uniform(key_off, (IFACE, IFACE), minval=-1.0, maxval=1.0) * (0.3 / math.sqrt(IFACE))
        return symmetric_block(noise, diagonal).astype(jnp.bfloat16)
    return lax.map(single, keys).reshape(DOFS, IFACE)


def draw_coarse_inverse(key, part):
    key = jax.random.fold_in(key, 17)
    key_diag, key_off = jax.random.split(key, 2)
    diagonal = jnp.exp(jax.random.uniform(key_diag, (COARSE,), minval=math.log(0.5), maxval=math.log(1.5)))
    noise = jax.random.uniform(key_off, (COARSE, COARSE), minval=-1.0, maxval=1.0) * (0.3 / math.sqrt(COARSE))
    return symmetric_block(noise, diagonal).astype(jnp.bfloat16)


def draw_loads(key, part):
    key = jax.random.fold_in(key, 5)
    key_base, key_spread = jax.random.split(key, 2)
    column = jnp.arange(DOFS)
    rise = 0.6 * 3.0 ** ((column // IFACE).astype(jnp.float32) / (SUBDOMAINS - 1))
    spread = jnp.exp(jax.random.uniform(key_spread, (DOFS,), minval=math.log(0.3), maxval=math.log(3.0)))
    base = jnp.clip(jax.random.normal(key_base, (CASES, DOFS)), -5.0, 5.0)
    return (base * spread[None, :] * rise[None, :]).astype(jnp.float32)


def shard_levels(key, dims, shards, low, largest):
    def one(dim, parts):
        draws = jax.random.uniform(jax.random.fold_in(jax.random.fold_in(key, 6), dim), (parts,), jnp.float32, low / len(shards), largest / len(shards))
        return jnp.repeat(jnp.exp(draws), dims[dim] // parts).reshape((-1,) + (1,) * (len(dims) - dim - 1))

    gain = one(*shards[0])
    for cut in shards[1:]:
        gain = gain * one(*cut)
    return gain


def bell_draw(key, shape, deviation, most, shards=(), held_as=jnp.bfloat16):
    factor_of = shard_levels(key, shape, shards, -0.22, 0.18) if shards else 1.0
    entries = jax.random.normal(key, shape, jnp.float32) * deviation * factor_of
    return jnp.minimum(jnp.maximum(entries, -most), most).astype(held_as)


def setup_inputs(seed: int = 0) -> dict:
    key_of = jax.random.split(jax.random.key(seed), 11)
    loads = draw_loads(jax.random.fold_in(key_of[10], 71), 0)
    stiffness = draw_stiffness(jax.random.fold_in(key_of[10], 71), 0)
    local_inverse = draw_local_inverse(jax.random.fold_in(key_of[10], 71), 0)
    coarse_basis = bell_draw(key_of[3], (PRIMAL, DOFS), IFACE ** -0.5, 0.1875, ((1, 256),))
    coarse_inverse = draw_coarse_inverse(jax.random.fold_in(key_of[10], 71), 0)
    primal_index = draw_primal_index(jax.random.fold_in(key_of[10], 71), 0)
    layer_counts = draw_layer_counts(jax.random.fold_in(key_of[10], 71), 0)
    layer_index = draw_layer_index(jax.random.fold_in(key_of[10], 71), 0)
    across_counts = draw_across_counts(jax.random.fold_in(key_of[10], 71), 0)
    across_index = draw_across_index(jax.random.fold_in(key_of[10], 71), 0)
    return {"loads": loads, "stiffness": stiffness, "local_inverse": local_inverse, "coarse_basis": coarse_basis, "coarse_inverse": coarse_inverse, "primal_index": primal_index, "layer_counts": layer_counts, "layer_index": layer_index, "across_counts": across_counts, "across_index": across_index}


def inner_product(left, right):
    return lax.dot_general(left.astype(jnp.float32), right.astype(jnp.float32), (((1,), (1,)), ((), ())), precision=lax.Precision.HIGHEST, preferred_element_type=jnp.float32)

def spd_solve(matrix, right_side):
    lower = jnp.linalg.cholesky(matrix)
    middle = lax.linalg.triangular_solve(lower, right_side, left_side=True, lower=True)
    return lax.linalg.triangular_solve(lower, middle, left_side=True, lower=True, transpose_a=True)

def take_rows(values, index):
    return jnp.take(values, index, axis=1)

def add_rows(values, index, extra):
    return values.at[:, index.reshape(-1)].add(extra.reshape(values.shape[0], -1))

def count_shared(layer_rows, layer_on, across_rows, across_on):
    shared = jnp.zeros((IFACE,), jnp.float32)
    shared = shared.at[layer_rows.reshape(-1)].add(layer_on.reshape(-1))
    shared = shared.at[across_rows.reshape(-1)].add(across_on.reshape(-1))
    return 1.0 / (1.0 + shared)

def assemble_all(vector, lists):
    layer_index, layer_mask, across_index, across_mask = lists
    local = vector.reshape(CASES, SUBDOMAINS, IFACE).transpose(1, 0, 2)
    layer_out = jax.vmap(take_rows)(local, layer_index) * layer_mask[:, None]
    layer_out = layer_out.reshape(LAYERS, ACROSS, CASES, 2, FACE_SLOTS)
    empty = jnp.zeros_like(layer_out[:1, :, :, 0])
    from_below = jnp.concatenate([empty, layer_out[:-1, :, :, 1]], 0).reshape(SUBDOMAINS, CASES, FACE_SLOTS)
    from_above = jnp.concatenate([layer_out[1:, :, :, 0], empty], 0).reshape(SUBDOMAINS, CASES, FACE_SLOTS)
    across_out = jax.vmap(take_rows)(local, across_index) * across_mask[:, None]
    across_out = across_out.reshape(LAYERS, ACROSS, CASES, ACROSS, SLOTS)
    arrived = jnp.transpose(across_out, (0, 3, 2, 1, 4)).reshape(SUBDOMAINS, CASES, ACROSS, SLOTS)
    summed = jax.vmap(add_rows)(local, across_index, arrived)
    summed = jax.vmap(add_rows)(summed, layer_index[:, 0], from_below)
    summed = jax.vmap(add_rows)(summed, layer_index[:, 1], from_above)
    return summed.transpose(1, 0, 2).reshape(CASES, DOFS)

def block_products(vector, blocks):
    local = vector.astype(jnp.bfloat16).reshape(CASES, SUBDOMAINS, IFACE).transpose(1, 0, 2)
    matrices = blocks.reshape(SUBDOMAINS, IFACE, IFACE)

    def single(operands):
        return jnp.dot(operands[0].astype(jnp.float32), operands[1].astype(jnp.float32), preferred_element_type=jnp.float32)
    return lax.map(single, (local, matrices)).transpose(1, 0, 2).reshape(CASES, DOFS)

def precondition(residual, weight, local_inverse, coarse_basis, coarse_inverse, primal_index, lists):
    weighted = (weight[None] * residual).astype(jnp.bfloat16)
    local_part = block_products(weighted, local_inverse)
    basis = coarse_basis.reshape(PRIMAL, SUBDOMAINS, IFACE).transpose(1, 0, 2)
    pieces = weighted.reshape(CASES, SUBDOMAINS, IFACE).transpose(1, 0, 2)

    def project(operands):
        return lax.dot_general(operands[0].astype(jnp.float32), operands[1].astype(jnp.float32), (((1,), (1,)), ((), ())), preferred_element_type=jnp.float32)
    terms = lax.map(project, (pieces, basis))
    coarse_rhs = jnp.zeros((CASES, COARSE), jnp.float32).at[:, primal_index.reshape(-1)].add(terms.transpose(1, 0, 2).reshape(CASES, -1))
    coarse_solution = lax.dot_general(coarse_rhs.astype(jnp.bfloat16).astype(jnp.float32), coarse_inverse.astype(jnp.float32), (((1,), (1,)), ((), ())), preferred_element_type=jnp.float32).astype(jnp.bfloat16)
    picked = jnp.take(coarse_solution, primal_index, axis=1).transpose(1, 0, 2)

    def expand(operands):
        return jnp.dot(operands[0].astype(jnp.float32), operands[1].astype(jnp.float32), preferred_element_type=jnp.float32)
    coarse_part = lax.map(expand, (picked, basis)).transpose(1, 0, 2).reshape(CASES, DOFS)
    return assemble_all(weight[None] * (local_part + coarse_part), lists)

def reference(loads, stiffness, local_inverse, coarse_basis, coarse_inverse, primal_index, layer_counts, layer_index, across_counts, across_index):
    layer_mask = (jnp.arange(FACE_SLOTS)[None, None, :] < layer_counts[:, :, None]).astype(jnp.float32)
    across_mask = (jnp.arange(SLOTS)[None, None, :] < across_counts[:, :, None]).astype(jnp.float32)
    weight = jax.vmap(count_shared)(layer_index, layer_mask, across_index, across_mask).reshape(DOFS)
    lists = (layer_index, layer_mask, across_index, across_mask)
    residual = assemble_all(loads, lists)
    solution = jnp.zeros_like(residual)
    precond = precondition(residual, weight, local_inverse, coarse_basis, coarse_inverse, primal_index, lists)
    product = inner_product(weight[None] * precond, residual)
    direction = precond
    for iteration in range(ITERS):
        image = assemble_all(block_products(direction, stiffness), lists)
        curvature = inner_product(weight[None] * direction, image)
        alpha = spd_solve(curvature, product)
        solution = solution + jnp.dot(alpha.T, direction, precision=lax.Precision.HIGHEST)
        residual = residual - jnp.dot(alpha.T, image, precision=lax.Precision.HIGHEST)
        precond = precondition(residual, weight, local_inverse, coarse_basis, coarse_inverse, primal_index, lists)
        product_next = inner_product(weight[None] * precond, residual)
        if iteration + 1 < ITERS:
            beta = spd_solve(product, product_next)
            direction = precond + jnp.dot(beta.T, direction, precision=lax.Precision.HIGHEST)
        product = product_next
    return (solution, residual, precond)
```

```python
import functools

import jax
import jax.numpy as jnp
from jax import lax
from jax.experimental import pallas as pl
from jax.experimental.pallas import tpu as pltpu
from jax.sharding import PartitionSpec as P

MESH = pl.DeviceIdType.MESH
F32, BF16 = jnp.float32, jnp.bfloat16

CASES = 16
IFACE = 1152
PRIMAL = 24
SLOTS = 48
FACE = 144
COARSE = 1024
RING = 16
TILES = 11
LANES = 128
NSLOT = TILES * LANES
PACKED = 512


def dot(a, b):
    return jnp.dot(a, b, preferred_element_type=F32)


def dot_nt(a, b):
    return lax.dot_general(a, b, (((1,), (1,)), ((), ())), preferred_element_type=F32)


def split(x):
    hi = x.astype(BF16)
    return hi, (x - hi.astype(F32)).astype(BF16)


def iota(shape, dim):
    return lax.broadcasted_iota(jnp.int32, shape, dim)


def fold(m):
    lane = iota((8, LANES), 1)
    return jnp.where(lane < 64, m[0:8], pltpu.roll(m[8:16], 64, 1))


def unfold(m):
    return jnp.concatenate([m, pltpu.roll(m, 64, 1)], axis=0)


def pack(tiles):
    lane = iota((8, LANES), 1)
    keep = (lane % 64) < 32
    pairs = []
    for i in range(8):
        even = jnp.where(keep, tiles[2 * i], 0.0)
        odd = jnp.where(keep, tiles[2 * i + 1], 0.0)
        pairs.append(even + pltpu.roll(odd, 32, 1))
    columns = []
    for i in range(4):
        a, b = pairs[2 * i], pairs[2 * i + 1]
        top = jnp.where(lane < 64, a, pltpu.roll(b, 64, 1))
        low = jnp.where(lane < 64, pltpu.roll(a, 64, 1), b)
        columns.append(jnp.concatenate([top, low], axis=0))
    return jnp.concatenate(columns, axis=1)


def eliminate(m, base):
    rows = iota((CASES, LANES), 0)
    for k in range(CASES):
        row = m[k : k + 1, :]
        scaled = row * (1.0 / row[:, base + k : base + k + 1])
        m = jnp.where(rows == k, scaled, m - m[:, base + k : base + k + 1] * scaled)
    return m


def lanes_of(m, start):
    lane = iota(m.shape, 1)
    return jnp.where((lane >= start) & (lane < start + CASES), m, 0.0)


def split3(x):
    a = x.astype(BF16)
    rest = x - a.astype(F32)
    b = rest.astype(BF16)
    return a, b, (rest - b.astype(F32)).astype(BF16)


def factor_t(m, start):
    a, b, c = (part.astype(F32) for part in split3(m))
    stack = jnp.concatenate([a, a, a, b, b, c, jnp.zeros((LANES - 6 * CASES, LANES), F32)], axis=0)
    return jnp.transpose(stack)[start : start + CASES, :].astype(BF16)


def apply_t(left, v):
    a, b, c = split3(v)
    pad = jnp.zeros((LANES - 6 * CASES, v.shape[1]), BF16)
    return dot(left, jnp.concatenate([a, b, c, a, b, a, pad], axis=0))


def kernel(
    loads, stiff_hbm, linv_hbm, basis, cinv_hbm, primal, lcounts, lindex, acounts, aindex,
    sol_out, res_out, pre_out,
    stiff, linv, cinv, gather, scatter, basis_rows, basis_cols, weight, table,
    idx, lidx, local, terms0, img,
    slot_s, slot_r, face_r, gram_s, gram_r, col_s, col_r, pk_s, pk_r, pidx_s, pidx_r, pcol_s, pcol_r,
    load_sem, slot_ss, slot_rs, face_ss, face_rs, gram_ss, gram_rs, col_ss, col_rs, pk_ss, pk_rs, px_ss, px_rs,
):
    gx, yz = lax.axis_index("gx"), lax.axis_index("yz")
    y, x = yz // 4, yz % 4
    offsets = sorted(
        [(a, b) for a in range(4) for b in range(4) if (a, b) != (0, 0)],
        key=lambda o: -(min(o[0], 4 - o[0]) + min(o[1], 4 - o[1])),
    )
    peers = [((y + a) % 4) * 4 + (x + b) % 4 for a, b in offsets]
    zs = sorted(range(1, RING), key=lambda o: -min(o, RING - o))
    columns = [(gx + o) % RING for o in zs]

    barrier = pltpu.get_barrier_semaphore()
    for q in peers:
        pl.semaphore_signal(barrier, 1, device_id=(gx, q), device_id_type=MESH)
    for q in columns:
        pl.semaphore_signal(barrier, 1, device_id=(q, yz), device_id_type=MESH)

    loading = [
        pltpu.make_async_copy(cinv_hbm, cinv, load_sem.at[0]),
        pltpu.make_async_copy(linv_hbm, linv, load_sem.at[1]),
        pltpu.make_async_copy(stiff_hbm, stiff, load_sem.at[2]),
    ]
    for copy in loading:
        copy.start()

    def to_peers(src, dst, ssem, rsem):
        for q in peers:
            pltpu.make_async_remote_copy(src(q), dst, ssem, rsem, device_id=(gx, q), device_id_type=MESH).start()

    def to_columns(src, dst, ssem, rsem):
        for q in columns:
            pltpu.make_async_remote_copy(src, dst, ssem, rsem, device_id=(q, yz), device_id_type=MESH).start()

    def wait_bytes(ref, sem):
        pltpu.make_async_copy(ref, ref, sem).wait()

    lane1 = iota((1, LANES), 1)
    idx[...] = jnp.full((LANES, LANES), -1, jnp.int32)
    lidx[...] = jnp.full((24, LANES), -1, jnp.int32)
    slot_lane = iota((1, SLOTS), 1)
    for q in range(RING):
        lidx[q : q + 1, 0:SLOTS] = jnp.where(slot_lane < acounts[0:1, q : q + 1], aindex[0, q : q + 1, :], -1)
    lane8 = iota((8, LANES), 1)
    idx[0:8, :] = jnp.where(lane8 < 64, lidx[0:8, :], pltpu.roll(lidx[8:16, :], 64, 1))
    face_lane = iota((1, FACE), 1)
    low = jnp.where(face_lane < lcounts[0:1, 0:1], lindex[0, 0:1, :], -1)
    up = jnp.where(face_lane < lcounts[0:1, 1:2], lindex[0, 1:2, :], -1)
    lidx[16:17, 0 : FACE - LANES] = low[:, LANES:FACE]
    lidx[17:18, 0 : FACE - LANES] = up[:, LANES:FACE]
    idx[8:9, :] = low[:, 0:LANES]
    idx[9:10, :] = jnp.where(lane1 < 64, lidx[16:17, :], pltpu.roll(lidx[17:18, :], 64, 1))
    idx[10:11, :] = up[:, 0:LANES]
    lidx[18:19, 0:PRIMAL] = primal[...]
    prow = lidx[18:19, :]

    row_iota = iota((IFACE, LANES), 0)
    for b in range(TILES):
        gather[:, b * LANES : (b + 1) * LANES] = jnp.where(row_iota == idx[b : b + 1, :], 1.0, 0.0).astype(BF16)
    idx_cols = jnp.transpose(idx[...].astype(F32))
    lane_iota = iota((LANES, IFACE), 1).astype(F32)
    for b in range(TILES):
        scatter[b * LANES : (b + 1) * LANES, :] = jnp.where(idx_cols[:, b : b + 1] == lane_iota, 1.0, 0.0).astype(BF16)
    weight[...] = 1.0 / (1.0 + dot(jnp.ones((CASES, NSLOT), BF16), scatter[...]))

    basis_pad = jnp.concatenate([basis[...].astype(F32), jnp.zeros((LANES - PRIMAL, IFACE), F32)], axis=0)
    basis_rows[...] = basis_pad.astype(BF16)
    basis_cols[...] = jnp.transpose(basis_pad).astype(BF16)

    prow8 = jnp.broadcast_to(prow.astype(F32), (8, LANES))
    pidx_s[...] = jnp.where(lane8 < 32, prow8, jnp.where((lane8 >= 64) & (lane8 < 96), pltpu.roll(prow8, 64, 1), 0.0))

    for phase in range(6):
        slot_r[phase, pl.ds(yz, 1)] = jnp.zeros((1, CASES, LANES), BF16)

    pl.semaphore_wait(barrier, len(peers) + len(columns))

    below, above = (gx + RING - 1) % RING, (gx + 1) % RING

    def exchange_start(phase, values):
        out = dot(values, gather[...]).astype(BF16)
        for b in range(TILES):
            slot_s[phase, b] = out[:, b * LANES : (b + 1) * LANES]
        to_peers(lambda q: slot_s.at[phase, q % 8], slot_r.at[phase, yz], slot_ss.at[phase], slot_rs.at[phase])
        pltpu.make_async_remote_copy(
            slot_s.at[phase, pl.ds(8, 2)], face_r.at[phase, 1], face_ss.at[phase], face_rs.at[phase],
            device_id=(below, yz), device_id_type=MESH,
        ).start()
        pltpu.make_async_remote_copy(
            slot_s.at[phase, pl.ds(9, 2)], face_r.at[phase, 0], face_ss.at[phase], face_rs.at[phase],
            device_id=(above, yz), device_id_type=MESH,
        ).start()

    def exchange_finish(phase):
        wait_bytes(face_r.at[phase], face_rs.at[phase])
        wait_bytes(slot_r.at[phase, pl.ds(0, 15)], slot_rs.at[phase])
        lane = iota((CASES, LANES), 1)
        first = yz < 8
        mine = (lane < 64) == first
        parts = []
        for b in range(8):
            a, c = slot_r[phase, b].astype(F32), slot_r[phase, b + 8].astype(F32)
            stay = jnp.where(first, a, c)
            move = jnp.where(first, c, a)
            parts.append(jnp.where(mine, stay, pltpu.roll(move, 64, 1)))
        parts.append(face_r[phase, 0, 1].astype(F32))
        tails = jnp.where(lane < 64, face_r[phase, 1, 1].astype(F32), face_r[phase, 0, 0].astype(F32))
        parts.append(pltpu.roll(tails, 64, 1))
        parts.append(face_r[phase, 1, 0].astype(F32))
        return dot(jnp.concatenate(parts, axis=1).astype(BF16), scatter[...])

    def coarse_terms(weighted):
        hi, lo = split(weighted)
        both = dot(jnp.concatenate([hi, lo], axis=0), basis_cols[...])
        return fold(both[0:CASES] + both[CASES:])

    def columns_start(phase, count):
        to_columns(
            col_s.at[phase, pl.ds(0, count)], col_r.at[phase, gx, pl.ds(0, count)], col_ss.at[phase], col_rs.at[phase]
        )

    def columns_wait(phase, count):
        wait_bytes(col_r.at[phase, pl.ds(0, 15), pl.ds(0, count)], col_rs.at[phase])

    def packed_start(phase, values):
        out = values.astype(BF16)
        pk_s[phase] = out
        pk_r[phase, pl.ds(yz, 1)] = out[None]
        to_peers(lambda q: pk_s.at[phase], pk_r.at[phase, yz], pk_ss.at[phase], pk_rs.at[phase])

    def coarse_finish(phase):
        wait_bytes(pk_r.at[phase, pl.ds(0, 15)], pk_rs.at[phase])
        everything = jnp.concatenate([pk_r[phase, q] for q in range(RING)], axis=1)
        picked = dot(everything, table[...]).astype(BF16)
        return weight[...] * (local[...] + dot(picked, basis_rows[...]))

    def grams(phase, z, others):
        z_hi, z_lo = split(z)
        highs, lows, at = [], [], 0
        for start, v in others:
            if start > at:
                highs.append(jnp.zeros((start - at, IFACE), BF16))
                lows.append(jnp.zeros((start - at, IFACE), BF16))
            hi, lo = split(v)
            highs.append(hi)
            lows.append(lo)
            at = start + CASES
        highs.append(jnp.zeros((LANES - at, IFACE), BF16))
        lows.append(jnp.zeros((LANES - at, IFACE), BF16))
        one = dot_nt(jnp.concatenate([z_hi, z_lo], axis=0), jnp.concatenate(highs, axis=0))
        two = dot_nt(z_hi, jnp.concatenate(lows, axis=0))
        mine = fold(one[0:CASES] + one[CASES:] + two)
        gram_s[phase] = mine
        gram_r[phase, pl.ds(yz, 1)] = mine[None]
        to_peers(lambda q: gram_s.at[phase], gram_r.at[phase, yz], gram_ss.at[phase], gram_rs.at[phase])

    def grams_layer(phase):
        wait_bytes(gram_r.at[phase, pl.ds(0, 15)], gram_rs.at[phase])
        return sum(gram_r[phase, q] for q in range(1, RING)) + gram_r[phase, 0]

    exchange_start(0, loads[...].astype(BF16))
    pcol_s_ref = pidx_s
    to_columns(pcol_s_ref, pidx_r.at[gx], px_ss.at[0], px_rs.at[0])
    pidx_r[pl.ds(gx, 1)] = pidx_s[...][None]
    loading[0].wait()
    chosen = jnp.where(iota((COARSE, LANES), 0) == prow, 1.0, 0.0).astype(BF16)
    inverse_cols = dot(cinv[...], chosen).astype(BF16)
    loading[1].wait()

    res = loads[...] + exchange_finish(0)
    weighted = weight[...] * res
    mine = coarse_terms(weighted)
    col_s[0, 0] = mine
    col_r[0, pl.ds(gx, 1), 0] = mine[None]
    columns_start(0, 1)
    wait_bytes(pidx_r.at[pl.ds(0, 15)], px_rs.at[0])
    owners = pack([pidx_r[g] for g in range(RING)])[0:8]
    pcol_s[...] = owners
    pcol_r[pl.ds(yz, 1)] = owners[None]
    to_peers(lambda q: pcol_s, pcol_r.at[yz], px_ss.at[1], px_rs.at[1])
    local[...] = dot(weighted.astype(BF16), linv[...])
    res_out[...] = res
    columns_wait(0, 1)
    packed = pack([col_r[0, g, 0] for g in range(RING)])
    packed_start(0, packed)
    terms0[...] = packed

    wait_bytes(pcol_r.at[pl.ds(0, 15)], px_rs.at[1])
    coarse_lane = iota((PACKED, COARSE), 1).astype(F32)

    def fill(p, carry):
        owner = jnp.transpose(pcol_r[p])
        one_hot = jnp.where(owner[:, 0:1] == coarse_lane, 1.0, 0.0).astype(BF16)
        table[pl.ds(pl.multiple_of(p * PACKED, PACKED), PACKED), :] = dot(one_hot, inverse_cols).astype(BF16)
        return carry

    lax.fori_loop(0, RING, fill, 0)

    t = coarse_finish(0)
    exchange_start(1, t.astype(BF16))
    loading[2].wait()
    z = t + exchange_finish(1)

    image = dot(z.astype(BF16), stiff[...])
    exchange_start(2, image.astype(BF16))
    grams(0, z, [(32, image), (48, weighted)])
    image = image + exchange_finish(2)
    mine = coarse_terms(weight[...] * image)
    layer = grams_layer(0)
    mine = jnp.where((lane8 % 64) < 32, mine, layer)
    col_s[1, 0] = mine
    col_r[1, pl.ds(gx, 1), 0] = mine[None]
    columns_start(1, 1)
    columns_wait(1, 1)
    tiles = [col_r[1, g, 0] for g in range(RING)]
    first = unfold(sum(tiles[1:]) + tiles[0])
    alpha = factor_t(eliminate(first, 32), 48)
    image_terms = pack(tiles)
    packed = terms0[...] - apply_t(alpha, image_terms)
    packed_start(1, packed)
    terms0[...] = packed
    res = res_out[...] - apply_t(alpha, image)
    weighted = weight[...] * res
    local[...] = dot(weighted.astype(BF16), linv[...])
    res_out[...] = res
    sol_out[...] = apply_t(alpha, z)
    pre_out[...] = z
    img[...] = image
    lane16 = iota((CASES, LANES), 1)
    identity = jnp.where(lane16 - 64 == iota((CASES, LANES), 0), 1.0, 0.0)
    inverse = lanes_of(eliminate(lanes_of(first, 48) + identity, 48), 64)
    t = coarse_finish(1)
    exchange_start(3, t.astype(BF16))
    z = t + exchange_finish(3)

    image = dot(z.astype(BF16), stiff[...])
    exchange_start(4, image.astype(BF16))
    grams(1, z, [(0, weight[...] * img[...]), (32, image), (48, weight[...] * res_out[...])])
    image = image + exchange_finish(4)
    mine = coarse_terms(weight[...] * image)
    layer = grams_layer(1)
    mine = jnp.where((lane8 % 64) < 32, mine, layer)
    col_s[2, 0] = mine
    col_s[2, 1] = layer
    col_r[2, pl.ds(gx, 1), 0] = mine[None]
    col_r[2, pl.ds(gx, 1), 1] = layer[None]
    columns_start(2, 2)
    columns_wait(2, 2)
    tiles = [col_r[2, g, 0] for g in range(RING)]
    second = unfold(sum(tiles[1:]) + tiles[0])
    cross = [col_r[2, g, 1] for g in range(RING)]
    cross = unfold(sum(cross[1:]) + cross[0])
    cross = jnp.concatenate([jnp.zeros((48, LANES), F32), cross, jnp.zeros((64, LANES), F32)], axis=0)
    cross_t = jnp.transpose(cross)[0:CASES, :]
    beta = apply_t(factor_t(inverse, 64), second)
    beta_t = factor_t(beta, 48)
    curve = apply_t(beta_t, cross_t + apply_t(factor_t(first, 32), beta))
    curve = curve + apply_t(factor_t(cross_t, 48), beta) + pltpu.roll(second, 16, 1)
    system = jnp.where(lane16 < 64, curve, pltpu.roll(second, 16, 1))
    alpha = factor_t(eliminate(system, 48), 64)
    new_terms = pack(tiles) + apply_t(beta_t, image_terms)
    packed_start(2, terms0[...] - apply_t(alpha, new_terms))
    image = image + apply_t(beta_t, img[...])
    res = res_out[...] - apply_t(alpha, image)
    local[...] = dot((weight[...] * res).astype(BF16), linv[...])
    res_out[...] = res
    direction = z + apply_t(beta_t, pre_out[...])
    sol_out[...] = sol_out[...] + apply_t(alpha, direction)
    t = coarse_finish(2)
    exchange_start(5, t.astype(BF16))
    pre_out[...] = t + exchange_finish(5)

    for phase in range(6):
        wait_bytes(slot_r.at[phase, pl.ds(0, 15)], slot_ss.at[phase])
        wait_bytes(face_r.at[phase], face_ss.at[phase])
    for phase in range(2):
        wait_bytes(gram_r.at[phase, pl.ds(0, 15)], gram_ss.at[phase])
    for phase in range(3):
        count = 2 if phase == 2 else 1
        wait_bytes(col_r.at[phase, pl.ds(0, 15), pl.ds(0, count)], col_ss.at[phase])
        wait_bytes(pk_r.at[phase, pl.ds(0, 15)], pk_ss.at[phase])
    wait_bytes(pidx_r.at[pl.ds(0, 15)], px_ss.at[0])
    wait_bytes(pcol_r.at[pl.ds(0, 15)], px_ss.at[1])


def per_device(*args):
    vector = jax.ShapeDtypeStruct((CASES, IFACE), F32)
    vmem = pl.BlockSpec(memory_space=pltpu.VMEM)
    hbm = pl.BlockSpec(memory_space=pl.ANY)
    dma = pltpu.SemaphoreType.DMA
    return pl.pallas_call(
        kernel,
        out_shape=(vector, vector, vector),
        in_specs=[vmem, hbm, hbm, vmem, hbm, vmem, vmem, vmem, vmem, vmem],
        out_specs=(vmem, vmem, vmem),
        scratch_shapes=[
            pltpu.VMEM((IFACE, IFACE), BF16),
            pltpu.VMEM((IFACE, IFACE), BF16),
            pltpu.VMEM((COARSE, COARSE), BF16),
            pltpu.VMEM((IFACE, NSLOT), BF16),
            pltpu.VMEM((NSLOT, IFACE), BF16),
            pltpu.VMEM((LANES, IFACE), BF16),
            pltpu.VMEM((IFACE, LANES), BF16),
            pltpu.VMEM((CASES, IFACE), F32),
            pltpu.VMEM((RING * PACKED, LANES), BF16),
            pltpu.VMEM((LANES, LANES), jnp.int32),
            pltpu.VMEM((24, LANES), jnp.int32),
            pltpu.VMEM((CASES, IFACE), F32),
            pltpu.VMEM((CASES, PACKED), F32),
            pltpu.VMEM((CASES, IFACE), F32),
            pltpu.VMEM((6, TILES, CASES, LANES), BF16),
            pltpu.VMEM((6, RING, CASES, LANES), BF16),
            pltpu.VMEM((6, 2, 2, CASES, LANES), BF16),
            pltpu.VMEM((2, 8, LANES), F32),
            pltpu.VMEM((2, RING, 8, LANES), F32),
            pltpu.VMEM((3, 2, 8, LANES), F32),
            pltpu.VMEM((3, RING, 2, 8, LANES), F32),
            pltpu.VMEM((3, CASES, PACKED), BF16),
            pltpu.VMEM((3, RING, CASES, PACKED), BF16),
            pltpu.VMEM((8, LANES), F32),
            pltpu.VMEM((RING, 8, LANES), F32),
            pltpu.VMEM((8, PACKED), F32),
            pltpu.VMEM((RING, 8, PACKED), F32),
            dma((3,)),
            dma((6,)), dma((6,)), dma((6,)), dma((6,)),
            dma((2,)), dma((2,)), dma((3,)), dma((3,)), dma((3,)), dma((3,)), dma((2,)), dma((2,)),
        ],
        compiler_params=pltpu.CompilerParams(
            collective_id=0, has_side_effects=True, vmem_limit_bytes=56 * 2**20
        ),
    )(*args)


def solution(mesh):
    whole = ("gx", "yz")
    columns, rows = P(None, whole), P(whole, None)
    lists = P(whole, None, None)
    return jax.shard_map(
        per_device,
        mesh=mesh,
        in_specs=(columns, rows, rows, columns, P(), rows, rows, lists, rows, lists),
        out_specs=(columns, columns, columns),
        check_vma=False,
    )
```

```python
import functools

import jax
import jax.numpy as jnp
from jax import lax
from jax.experimental import pallas as pl
from jax.experimental.pallas import tpu as pltpu
from jax.sharding import PartitionSpec as P

MESH = pl.DeviceIdType.MESH
F32, BF16 = jnp.float32, jnp.bfloat16

CASES = 16
IFACE = 1152
PRIMAL = 24
SLOTS = 48
FACE = 144
COARSE = 1024
RING = 16
TILES = 11
LANES = 128
NSLOT = TILES * LANES
PACKED = 512
HALF = 512
BLOCK = 32
EXT = 640


def dot(a, b):
    return jnp.dot(a, b, preferred_element_type=F32)


def dot_nt(a, b):
    return lax.dot_general(a, b, (((1,), (1,)), ((), ())), preferred_element_type=F32)


def split(x):
    hi = x.astype(BF16)
    return hi, (x - hi.astype(F32)).astype(BF16)


def iota(shape, dim):
    return lax.broadcasted_iota(jnp.int32, shape, dim)


def fold(m):
    lane = iota((8, LANES), 1)
    return jnp.where(lane < 64, m[0:8], pltpu.roll(m[8:16], 64, 1))


def unfold(m):
    return jnp.concatenate([m, pltpu.roll(m, 64, 1)], axis=0)


def pack(tiles):
    lane = iota((8, LANES), 1)
    keep = (lane % 64) < 32
    pairs = []
    for i in range(8):
        even = jnp.where(keep, tiles[2 * i], 0.0)
        odd = jnp.where(keep, tiles[2 * i + 1], 0.0)
        pairs.append(even + pltpu.roll(odd, 32, 1))
    columns = []
    for i in range(4):
        a, b = pairs[2 * i], pairs[2 * i + 1]
        top = jnp.where(lane < 64, a, pltpu.roll(b, 64, 1))
        low = jnp.where(lane < 64, pltpu.roll(a, 64, 1), b)
        columns.append(jnp.concatenate([top, low], axis=0))
    return jnp.concatenate(columns, axis=1)


def eliminate(m, base):
    rows = iota((CASES, LANES), 0)
    for k in range(CASES):
        row = m[k : k + 1, :]
        scaled = row * (1.0 / row[:, base + k : base + k + 1])
        m = jnp.where(rows == k, scaled, m - m[:, base + k : base + k + 1] * scaled)
    return m


def lanes_of(m, start):
    lane = iota(m.shape, 1)
    return jnp.where((lane >= start) & (lane < start + CASES), m, 0.0)


def split3(x):
    a = x.astype(BF16)
    rest = x - a.astype(F32)
    b = rest.astype(BF16)
    return a, b, (rest - b.astype(F32)).astype(BF16)


def factor_t(m, start):
    a, b, c = (part.astype(F32) for part in split3(m))
    stack = jnp.concatenate([a, a, a, b, b, c, jnp.zeros((LANES - 6 * CASES, LANES), F32)], axis=0)
    return jnp.transpose(stack)[start : start + CASES, :].astype(BF16)


def apply_t(left, v):
    a, b, c = split3(v)
    pad = jnp.zeros((LANES - 6 * CASES, v.shape[1]), BF16)
    return dot(left, jnp.concatenate([a, b, c, a, b, a, pad], axis=0))


def kernel(
    loads, stiff_hbm, linv_hbm, basis, cinv_hbm, primal, lcounts, lindex, acounts, aindex,
    sol_out, res_out, pre_out,
    stiff, linv, cinv, gather, scatter, basis_cols, weight, spread, near, near_inverse,
    idx, lidx, smooth, terms0, img, img_smooth,
    slot_s, slot_r, face_r, wide_s, wide_r, wface_r, gram_s, gram_r, col_s, col_r,
    half_s, half_r, sib_s, sib_r, pidx_s, pidx_rp, pidx_rc,
    load_sem, slot_ss, slot_rs, face_ss, face_rs, wide_ss, wide_rs, wface_ss, wface_rs,
    gram_ss, gram_rs, col_ss, col_rs, half_ss, half_rs, sib_ss, sib_rs, px_ss, px_rs,
):
    gx, yz = lax.axis_index("gx"), lax.axis_index("yz")
    y, x = yz // 4, yz % 4
    offsets = sorted(
        [(a, b) for a in range(4) for b in range(4) if (a, b) != (0, 0)],
        key=lambda o: -(min(o[0], 4 - o[0]) + min(o[1], 4 - o[1])),
    )
    peers = [((y + a) % 4) * 4 + (x + b) % 4 for a, b in offsets]
    zs = sorted(range(1, RING), key=lambda o: -min(o, RING - o))
    columns = [(gx + o) % RING for o in zs]
    below, above = (gx + RING - 1) % RING, (gx + 1) % RING
    core = gx % 2
    sibling = gx + 1 - 2 * core

    barrier = pltpu.get_barrier_semaphore()
    for q in peers:
        pl.semaphore_signal(barrier, 1, device_id=(gx, q), device_id_type=MESH)
    for q in columns:
        pl.semaphore_signal(barrier, 1, device_id=(q, yz), device_id_type=MESH)

    loading = [
        pltpu.make_async_copy(linv_hbm, linv, load_sem.at[0]),
        pltpu.make_async_copy(cinv_hbm, cinv, load_sem.at[1]),
        pltpu.make_async_copy(stiff_hbm, stiff, load_sem.at[2]),
    ]
    for copy in loading:
        copy.start()

    sent = []

    def wait_bytes(ref, sem):
        pltpu.make_async_copy(ref, ref, sem).wait()

    def send(src, dst, ssem, rsem, device):
        pltpu.make_async_remote_copy(src, dst, ssem, rsem, device_id=device, device_id_type=MESH).start()

    def to_peers(src, dst, arrivals, ssem, rsem):
        for q in peers:
            send(src(q), dst, ssem, rsem, (gx, q))
        sent.append((arrivals, ssem))

    def to_columns(src, dst, arrivals, ssem, rsem):
        for q in columns:
            send(src, dst, ssem, rsem, (q, yz))
        sent.append((arrivals, ssem))

    lane1 = iota((1, LANES), 1)
    lane8 = iota((8, LANES), 1)
    lane16 = iota((CASES, LANES), 1)
    idx[...] = jnp.full((LANES, LANES), -1, jnp.int32)
    lidx[...] = jnp.full((24, LANES), -1, jnp.int32)
    slot_lane = iota((1, SLOTS), 1)
    for q in range(RING):
        lidx[q : q + 1, 0:SLOTS] = jnp.where(slot_lane < acounts[0:1, q : q + 1], aindex[0, q : q + 1, :], -1)
    idx[0:8, :] = jnp.where(lane8 < 64, lidx[0:8, :], pltpu.roll(lidx[8:16, :], 64, 1))
    face_lane = iota((1, FACE), 1)
    low = jnp.where(face_lane < lcounts[0:1, 0:1], lindex[0, 0:1, :], -1)
    up = jnp.where(face_lane < lcounts[0:1, 1:2], lindex[0, 1:2, :], -1)
    lidx[16:17, 0 : FACE - LANES] = low[:, LANES:FACE]
    lidx[17:18, 0 : FACE - LANES] = up[:, LANES:FACE]
    idx[8:9, :] = low[:, 0:LANES]
    idx[9:10, :] = jnp.where(lane1 < 64, lidx[16:17, :], pltpu.roll(lidx[17:18, :], 64, 1))
    idx[10:11, :] = up[:, 0:LANES]
    lidx[18:19, 0:PRIMAL] = primal[...]
    row_iota = iota((IFACE, LANES), 0)
    for b in range(TILES):
        gather[:, b * LANES : (b + 1) * LANES] = jnp.where(row_iota == idx[b : b + 1, :], 1.0, 0.0).astype(BF16)

    def exchange_values(sends, phase, values):
        out = dot(values, gather[...]).astype(BF16)
        for b in range(TILES):
            sends[phase, b] = out[:, b * LANES : (b + 1) * LANES]

    def exchange_send(phase, sends, arrived, faces, ss, rs, fss, frs):
        to_peers(
            lambda q: sends.at[phase, q % 8], arrived.at[phase, yz], arrived.at[phase, pl.ds(0, 15)],
            ss.at[phase], rs.at[phase],
        )
        send(sends.at[phase, pl.ds(8, 2)], faces.at[phase, 1], fss.at[phase], frs.at[phase], (below, yz))
        send(sends.at[phase, pl.ds(9, 2)], faces.at[phase, 0], fss.at[phase], frs.at[phase], (above, yz))
        sent.append((faces.at[phase], fss.at[phase]))

    def exchange_arrived(phase, arrived, faces, rs, frs):
        wait_bytes(faces.at[phase], frs.at[phase])
        wait_bytes(arrived.at[phase, pl.ds(0, 15)], rs.at[phase])
        lane = iota(arrived.shape[2:], 1)
        first = yz < 8
        mine = (lane < 64) == first
        parts = []
        for b in range(8):
            a, c = arrived[phase, b].astype(F32), arrived[phase, b + 8].astype(F32)
            stay = jnp.where(first, a, c)
            move = jnp.where(first, c, a)
            parts.append(jnp.where(mine, stay, pltpu.roll(move, 64, 1)))
        parts.append(faces[phase, 0, 1].astype(F32))
        tails = jnp.where(lane < 64, faces[phase, 1, 1].astype(F32), faces[phase, 0, 0].astype(F32))
        parts.append(pltpu.roll(tails, 64, 1))
        parts.append(faces[phase, 1, 0].astype(F32))
        return parts

    def exchange_start(phase, values):
        exchange_values(slot_s, phase, values)
        exchange_send(phase, slot_s, slot_r, face_r, slot_ss, slot_rs, face_ss, face_rs)

    def exchange_finish(phase):
        parts = exchange_arrived(phase, slot_r, face_r, slot_rs, face_rs)
        return dot(jnp.concatenate(parts, axis=1).astype(BF16), scatter[...])

    def wide_start(phase, values):
        exchange_values(wide_s, phase, values)
        exchange_send(phase, wide_s, wide_r, wface_r, wide_ss, wide_rs, wface_ss, wface_rs)

    def smooth_start(phase, weighted):
        hi, lo = split(weighted)
        both = dot(jnp.concatenate([hi, lo], axis=0), linv[...])
        part = weight[...] * (both[0:CASES] + both[CASES:])
        hi, lo = split(part)
        wide_start(phase, jnp.concatenate([hi, lo], axis=0))
        return part

    def smooth_finish(phase):
        parts = exchange_arrived(phase, wide_r, wface_r, wide_rs, wface_rs)
        both = dot(jnp.concatenate(parts, axis=1).astype(BF16), scatter[...])
        return both[0:CASES] + both[CASES:]

    def coarse_terms(weighted):
        hi, lo = split(weighted)
        both = dot(jnp.concatenate([hi, lo], axis=0), basis_cols[...])
        return fold(both[0:CASES] + both[CASES:])

    def columns_start(phase, count):
        to_columns(
            col_s.at[phase, pl.ds(0, count)], col_r.at[phase, gx, pl.ds(0, count)],
            col_r.at[phase, pl.ds(0, 15), pl.ds(0, count)], col_ss.at[phase], col_rs.at[phase],
        )

    def columns_wait(phase, count):
        wait_bytes(col_r.at[phase, pl.ds(0, 15), pl.ds(0, count)], col_rs.at[phase])

    def coarse_start(phase, packed):
        hi, lo = split(packed)
        both = dot(jnp.concatenate([hi, lo], axis=0), spread[...])
        out = (both[0:CASES] + both[CASES:]).astype(BF16)
        half_s[phase] = out
        half_r[phase, pl.ds(yz, 1)] = out[None]
        arrivals = half_r.at[phase, pl.ds(0, 15)]
        to_peers(lambda q: half_s.at[phase], half_r.at[phase, yz], arrivals, half_ss.at[phase], half_rs.at[phase])

    def coarse_finish(phase):
        wait_bytes(half_r.at[phase, pl.ds(0, 15)], half_rs.at[phase])
        total = half_r[phase, 0].astype(F32)
        for q in range(1, RING):
            total = total + half_r[phase, q].astype(F32)
        sib_s[phase] = total
        send(sib_s.at[phase], sib_r.at[phase], sib_ss.at[phase], sib_rs.at[phase], (sibling, yz))
        sent.append((sib_s.at[phase], sib_ss.at[phase]))
        own = pl.ds(pl.multiple_of(core * HALF, HALF), HALF)
        other = pl.ds(pl.multiple_of((1 - core) * HALF, HALF), HALF)
        picked = dot(total.astype(BF16), near_inverse[own, :])
        wait_bytes(sib_r.at[phase], sib_rs.at[phase])
        picked = picked + dot(sib_r[phase].astype(BF16), near_inverse[other, :])
        return dot(picked.astype(BF16), near[...])

    def grams(phase, z, others):
        z_hi, z_lo = split(z)
        highs, lows, at = [], [], 0
        for start, v in others:
            if start > at:
                highs.append(jnp.zeros((start - at, IFACE), BF16))
                lows.append(jnp.zeros((start - at, IFACE), BF16))
            hi, lo = split(v)
            highs.append(hi)
            lows.append(lo)
            at = start + CASES
        highs.append(jnp.zeros((LANES - at, IFACE), BF16))
        lows.append(jnp.zeros((LANES - at, IFACE), BF16))
        one = dot_nt(jnp.concatenate([z_hi, z_lo], axis=0), jnp.concatenate(highs, axis=0))
        two = dot_nt(z_hi, jnp.concatenate(lows, axis=0))
        mine = fold(one[0:CASES] + one[CASES:] + two)
        gram_s[phase] = mine
        gram_r[phase, pl.ds(yz, 1)] = mine[None]
        arrivals = gram_r.at[phase, pl.ds(0, 15)]
        to_peers(lambda q: gram_s.at[phase], gram_r.at[phase, yz], arrivals, gram_ss.at[phase], gram_rs.at[phase])

    def grams_layer(phase):
        wait_bytes(gram_r.at[phase, pl.ds(0, 15)], gram_rs.at[phase])
        return sum(gram_r[phase, q] for q in range(1, RING)) + gram_r[phase, 0]

    for phase in range(3):
        slot_r[phase, pl.ds(yz, 1)] = jnp.zeros((1, CASES, LANES), BF16)
    for phase in range(4):
        wide_r[phase, pl.ds(yz, 1)] = jnp.zeros((1, BLOCK, LANES), BF16)
    prow8 = jnp.broadcast_to(lidx[18:19, :].astype(F32), (8, LANES))
    primals = jnp.where(lane8 < 32, prow8, jnp.where((lane8 >= 64) & (lane8 < 96), pltpu.roll(prow8, 64, 1), 0.0))
    pidx_s[...] = primals
    pidx_rp[pl.ds(yz, 1)] = primals[None]
    pidx_rc[pl.ds(gx, 1)] = primals[None]
    exchange_values(slot_s, 0, loads[...].astype(BF16))

    pl.semaphore_wait(barrier, len(peers) + len(columns))

    exchange_send(0, slot_s, slot_r, face_r, slot_ss, slot_rs, face_ss, face_rs)
    to_columns(pidx_s, pidx_rc.at[gx], pidx_rc.at[pl.ds(0, 15)], px_ss.at[0], px_rs.at[0])
    to_peers(lambda q: pidx_s, pidx_rp.at[yz], pidx_rp.at[pl.ds(0, 15)], px_ss.at[1], px_rs.at[1])
    idx_cols = jnp.transpose(idx[...].astype(F32))
    lane_iota = iota((LANES, IFACE), 1).astype(F32)
    for b in range(TILES):
        scatter[b * LANES : (b + 1) * LANES, :] = jnp.where(idx_cols[:, b : b + 1] == lane_iota, 1.0, 0.0).astype(BF16)
    weight[...] = 1.0 / (1.0 + dot(jnp.ones((CASES, NSLOT), BF16), scatter[...]))
    basis_f32 = basis[...].astype(F32)
    basis_pad = jnp.concatenate([basis_f32, jnp.zeros((LANES - PRIMAL, IFACE), F32)], axis=0)
    basis_cols[...] = jnp.transpose(basis_pad).astype(BF16)
    scaled = jnp.concatenate([weight[...] * basis_pad[0:CASES], weight[...] * basis_pad[CASES:BLOCK]], axis=0)
    scaled = scaled.astype(BF16)
    wide_start(3, scaled)
    loading[0].wait()

    res = loads[...] + exchange_finish(0)
    weighted = weight[...] * res
    mine = coarse_terms(weighted)
    col_s[0, 0] = mine
    col_r[0, pl.ds(gx, 1), 0] = mine[None]
    columns_start(0, 1)
    own_smooth = smooth_start(0, weighted)
    res_out[...] = res

    wait_bytes(pidx_rc.at[pl.ds(0, 15)], px_rs.at[0])
    owners = jnp.transpose(pack([pidx_rc[g] for g in range(RING)])[0:8])
    half_lane = (iota((PACKED, HALF), 1) + core * HALF).astype(F32)
    spread[...] = jnp.where(owners[:, 0:1] == half_lane, 1.0, 0.0).astype(BF16)
    columns_wait(0, 1)
    packed = pack([col_r[0, g, 0] for g in range(RING)])
    coarse_start(0, packed)
    terms0[...] = packed

    wait_bytes(pidx_rp.at[pl.ds(0, 15)], px_rs.at[1])
    across_primals = pack([pidx_rp[q] for q in range(RING)])[0:8]
    lower = pidx_rc[pl.ds(below, 1)][0]
    upper = pltpu.roll(pidx_rc[pl.ds(above, 1)][0], 32, 1)
    face_primals = jnp.where(lane8 < 32, lower, jnp.where(lane8 < 64, upper, -1.0))
    near_row = jnp.concatenate([across_primals, face_primals], axis=1)[0:1]
    chosen = jnp.where(iota((COARSE, EXT), 0).astype(F32) == near_row, 1.0, 0.0).astype(BF16)
    loading[1].wait()
    near_inverse[...] = dot(cinv[...], chosen).astype(BF16)

    parts = exchange_arrived(3, wide_r, wface_r, wide_rs, wface_rs)
    lane32 = iota((BLOCK, LANES), 1)
    for b in range(8):
        both = jnp.concatenate([jnp.where(lane32 < 64, parts[b], 0.0), jnp.where(lane32 < 64, 0.0, parts[b])], axis=0)
        rows = dot(both.astype(BF16), scatter[b * LANES : (b + 1) * LANES, :]).astype(BF16)
        near[b * BLOCK : (b + 1) * BLOCK, :] = rows[0:BLOCK]
        near[(b + 8) * BLOCK : (b + 9) * BLOCK, :] = rows[BLOCK:]
    none = jnp.zeros((BLOCK, LANES), F32)
    faces = jnp.concatenate([
        jnp.concatenate([parts[8], jnp.where(lane32 < 64, parts[9], 0.0), none], axis=1),
        jnp.concatenate([none, jnp.where(lane32 < 64, 0.0, parts[9]), parts[10]], axis=1),
    ], axis=0)
    near[16 * BLOCK : 18 * BLOCK, :] = dot(faces.astype(BF16), scatter[8 * LANES :, :]).astype(BF16)
    near[18 * BLOCK :, :] = jnp.zeros((EXT - 18 * BLOCK, IFACE), BF16)
    near[pl.ds(pl.multiple_of(yz * BLOCK, BLOCK), BLOCK), :] = scaled

    own_smooth = own_smooth + smooth_finish(0)
    smooth[...] = own_smooth
    loading[2].wait()
    z = own_smooth + coarse_finish(0)

    image = dot(z.astype(BF16), stiff[...])
    exchange_start(1, image.astype(BF16))
    grams(0, z, [(32, image), (48, weighted)])
    image = image + exchange_finish(1)
    weighted = weight[...] * image
    mine = coarse_terms(weighted)
    mine = jnp.where((lane8 % 64) < 32, mine, grams_layer(0))
    col_s[1, 0] = mine
    col_r[1, pl.ds(gx, 1), 0] = mine[None]
    columns_start(1, 1)
    own_smooth = smooth_start(1, weighted)
    img[...] = image
    columns_wait(1, 1)
    tiles = [col_r[1, g, 0] for g in range(RING)]
    first = unfold(sum(tiles[1:]) + tiles[0])
    image_terms = pack(tiles)
    alpha = factor_t(eliminate(first, 32), 48)
    packed = terms0[...] - apply_t(alpha, image_terms)
    coarse_start(1, packed)
    terms0[...] = packed
    res_out[...] = res_out[...] - apply_t(alpha, image)
    sol_out[...] = apply_t(alpha, z)
    pre_out[...] = z
    identity = jnp.where(lane16 - 64 == iota((CASES, LANES), 0), 1.0, 0.0)
    inverse = eliminate(lanes_of(first, 48) + identity, 48)
    own_smooth = own_smooth + smooth_finish(1)
    img_smooth[...] = own_smooth
    own_smooth = smooth[...] - apply_t(alpha, own_smooth)
    smooth[...] = own_smooth
    z = own_smooth + coarse_finish(1)

    image = dot(z.astype(BF16), stiff[...])
    exchange_start(2, image.astype(BF16))
    grams(1, z, [(0, weight[...] * img[...]), (32, image), (48, weight[...] * res_out[...])])
    image = image + exchange_finish(2)
    weighted = weight[...] * image
    mine = coarse_terms(weighted)
    layer = grams_layer(1)
    mine = jnp.where((lane8 % 64) < 32, mine, layer)
    col_s[2, 0] = mine
    col_s[2, 1] = layer
    col_r[2, pl.ds(gx, 1), 0] = mine[None]
    col_r[2, pl.ds(gx, 1), 1] = layer[None]
    columns_start(2, 2)
    own_smooth = smooth_start(2, weighted)
    columns_wait(2, 2)
    tiles = [col_r[2, g, 0] for g in range(RING)]
    second = unfold(sum(tiles[1:]) + tiles[0])
    cross = [col_r[2, g, 1] for g in range(RING)]
    cross = unfold(sum(cross[1:]) + cross[0])
    cross = jnp.concatenate([jnp.zeros((48, LANES), F32), cross, jnp.zeros((64, LANES), F32)], axis=0)
    cross_t = jnp.transpose(cross)[0:CASES, :]
    beta = apply_t(factor_t(inverse, 64), second)
    beta_t = factor_t(beta, 48)
    curve = apply_t(beta_t, cross_t + apply_t(factor_t(first, 32), beta))
    curve = curve + apply_t(factor_t(cross_t, 48), beta) + pltpu.roll(second, 16, 1)
    system = jnp.where(lane16 < 64, curve, pltpu.roll(second, 16, 1))
    new_terms = pack(tiles) + apply_t(beta_t, image_terms)
    alpha = factor_t(eliminate(system, 48), 64)
    coarse_start(2, terms0[...] - apply_t(alpha, new_terms))
    image = image + apply_t(beta_t, img[...])
    res_out[...] = res_out[...] - apply_t(alpha, image)
    direction = z + apply_t(beta_t, pre_out[...])
    sol_out[...] = sol_out[...] + apply_t(alpha, direction)
    own_smooth = own_smooth + smooth_finish(2) + apply_t(beta_t, img_smooth[...])
    own_smooth = smooth[...] - apply_t(alpha, own_smooth)
    pre_out[...] = own_smooth + coarse_finish(2)

    for arrivals, ssem in sent:
        wait_bytes(arrivals, ssem)


def hand_over(a, b, c, a_out, b_out, c_out, sems):
    copies = [
        pltpu.make_async_copy(src, dst, sems.at[i])
        for i, (src, dst) in enumerate([(a, a_out), (b, b_out), (c, c_out)])
    ]
    for copy in copies:
        copy.start()
    for copy in copies:
        copy.wait()


def per_device(*args):
    vector = jax.ShapeDtypeStruct((CASES, IFACE), F32)
    vmem = pl.BlockSpec(memory_space=pltpu.VMEM)
    hbm = pl.BlockSpec(memory_space=pl.ANY)
    dma = pltpu.SemaphoreType.DMA
    results = pl.pallas_call(
        kernel,
        out_shape=(vector, vector, vector),
        in_specs=[vmem, hbm, hbm, vmem, hbm, vmem, vmem, vmem, vmem, vmem],
        out_specs=(vmem, vmem, vmem),
        scratch_shapes=[
            pltpu.VMEM((IFACE, IFACE), BF16),
            pltpu.VMEM((IFACE, IFACE), BF16),
            pltpu.VMEM((COARSE, COARSE), BF16),
            pltpu.VMEM((IFACE, NSLOT), BF16),
            pltpu.VMEM((NSLOT, IFACE), BF16),
            pltpu.VMEM((IFACE, LANES), BF16),
            pltpu.VMEM((CASES, IFACE), F32),
            pltpu.VMEM((PACKED, HALF), BF16),
            pltpu.VMEM((EXT, IFACE), BF16),
            pltpu.VMEM((COARSE, EXT), BF16),
            pltpu.VMEM((LANES, LANES), jnp.int32),
            pltpu.VMEM((24, LANES), jnp.int32),
            pltpu.VMEM((CASES, IFACE), F32),
            pltpu.VMEM((CASES, PACKED), F32),
            pltpu.VMEM((CASES, IFACE), F32),
            pltpu.VMEM((CASES, IFACE), F32),
            pltpu.VMEM((3, TILES, CASES, LANES), BF16),
            pltpu.VMEM((3, RING, CASES, LANES), BF16),
            pltpu.VMEM((3, 2, 2, CASES, LANES), BF16),
            pltpu.VMEM((4, TILES, BLOCK, LANES), BF16),
            pltpu.VMEM((4, RING, BLOCK, LANES), BF16),
            pltpu.VMEM((4, 2, 2, BLOCK, LANES), BF16),
            pltpu.VMEM((2, 8, LANES), F32),
            pltpu.VMEM((2, RING, 8, LANES), F32),
            pltpu.VMEM((3, 2, 8, LANES), F32),
            pltpu.VMEM((3, RING, 2, 8, LANES), F32),
            pltpu.VMEM((3, CASES, HALF), BF16),
            pltpu.VMEM((3, RING, CASES, HALF), BF16),
            pltpu.VMEM((3, CASES, HALF), F32),
            pltpu.VMEM((3, CASES, HALF), F32),
            pltpu.VMEM((8, LANES), F32),
            pltpu.VMEM((RING, 8, LANES), F32),
            pltpu.VMEM((RING, 8, LANES), F32),
            dma((3,)),
            dma((3,)), dma((3,)), dma((3,)), dma((3,)),
            dma((4,)), dma((4,)), dma((4,)), dma((4,)),
            dma((2,)), dma((2,)), dma((3,)), dma((3,)),
            dma((3,)), dma((3,)), dma((3,)), dma((3,)), dma((2,)), dma((2,)),
        ],
        compiler_params=pltpu.CompilerParams(
            collective_id=0, has_side_effects=True, vmem_limit_bytes=56 * 2**20
        ),
    )(*args)
    return pl.pallas_call(
        hand_over,
        out_shape=(vector, vector, vector),
        in_specs=[hbm, hbm, hbm],
        out_specs=(hbm, hbm, hbm),
        scratch_shapes=[dma((3,))],
        compiler_params=pltpu.CompilerParams(vmem_limit_bytes=60 * 2**20),
    )(*results)


def solution(mesh):
    whole = ("gx", "yz")
    columns, rows = P(None, whole), P(whole, None)
    lists = P(whole, None, None)
    return jax.shard_map(
        per_device,
        mesh=mesh,
        in_specs=(columns, rows, rows, columns, P(), rows, rows, lists, rows, lists),
        out_specs=(columns, columns, columns),
        check_vma=False,
    )
```

```python
import functools

import jax
import jax.numpy as jnp
from jax import lax
from jax.experimental import pallas as pl
from jax.experimental.pallas import tpu as pltpu
from jax.sharding import PartitionSpec as P

MESH = pl.DeviceIdType.MESH
F32, BF16 = jnp.float32, jnp.bfloat16

CASES = 16
IFACE = 1152
PRIMAL = 24
SLOTS = 48
FACE = 144
COARSE = 1024
RING = 16
TILES = 11
LANES = 128
NSLOT = TILES * LANES
PACKED = 512
HALF = 512
BLOCK = 32
EXT = 640


def dot(a, b):
    return jnp.dot(a, b, preferred_element_type=F32)


def dot_nt(a, b):
    return lax.dot_general(a, b, (((1,), (1,)), ((), ())), preferred_element_type=F32)


def split(x):
    hi = x.astype(BF16)
    return hi, (x - hi.astype(F32)).astype(BF16)


def iota(shape, dim):
    return lax.broadcasted_iota(jnp.int32, shape, dim)


def fold(m):
    lane = iota((8, LANES), 1)
    return jnp.where(lane < 64, m[0:8], pltpu.roll(m[8:16], 64, 1))


def unfold(m):
    return jnp.concatenate([m, pltpu.roll(m, 64, 1)], axis=0)


def pack(tiles):
    lane = iota((8, LANES), 1)
    keep = (lane % 64) < 32
    pairs = []
    for i in range(8):
        even = jnp.where(keep, tiles[2 * i], 0.0)
        odd = jnp.where(keep, tiles[2 * i + 1], 0.0)
        pairs.append(even + pltpu.roll(odd, 32, 1))
    columns = []
    for i in range(4):
        a, b = pairs[2 * i], pairs[2 * i + 1]
        top = jnp.where(lane < 64, a, pltpu.roll(b, 64, 1))
        low = jnp.where(lane < 64, pltpu.roll(a, 64, 1), b)
        columns.append(jnp.concatenate([top, low], axis=0))
    return jnp.concatenate(columns, axis=1)


def eliminate(m, base):
    rows = iota((CASES, LANES), 0)
    for k in range(CASES):
        row = m[k : k + 1, :]
        scaled = row * (1.0 / row[:, base + k : base + k + 1])
        m = jnp.where(rows == k, scaled, m - m[:, base + k : base + k + 1] * scaled)
    return m


def lanes_of(m, start):
    lane = iota(m.shape, 1)
    return jnp.where((lane >= start) & (lane < start + CASES), m, 0.0)


def split3(x):
    a = x.astype(BF16)
    rest = x - a.astype(F32)
    b = rest.astype(BF16)
    return a, b, (rest - b.astype(F32)).astype(BF16)


def factor_t(m, start):
    a, b, c = (part.astype(F32) for part in split3(m))
    stack = jnp.concatenate([a, a, a, b, b, c, jnp.zeros((LANES - 6 * CASES, LANES), F32)], axis=0)
    return jnp.transpose(stack)[start : start + CASES, :].astype(BF16)


def apply_t(left, v):
    a, b, c = split3(v)
    pad = jnp.zeros((LANES - 6 * CASES, v.shape[1]), BF16)
    return dot(left, jnp.concatenate([a, b, c, a, b, a, pad], axis=0))


def kernel(
    loads, stiff_hbm, linv_hbm, basis, cinv_hbm, primal, lcounts, lindex, acounts, aindex,
    sol_out, res_out, pre_out,
    stiff, linv, cinv, gather, scatter, basis_cols, weight, spread, near, near_t, chosen_t, near_inverse,
    idx, lidx, smooth, rhs, img, img_smooth, img_rhs,
    slot_s, slot_r, face_r, wide_s, wide_r, wface_r, gram_s, gram_r, ring_s, ring_r, col_s, col_r,
    half_s, half_r, sib_s, sib_r, part_s, part_r, sum_s, sum_r, all_s, all_r, pidx_s, pidx_rp, pidx_rc,
    load_sem, slot_ss, slot_rs, face_ss, face_rs, wide_ss, wide_rs, wface_ss, wface_rs,
    gram_ss, gram_rs, ring_ss, ring_rs, part_ss, part_rs, sum_ss, sum_rs, all_ss, all_rs, one_ss, one_rs,
):
    gx, yz = lax.axis_index("gx"), lax.axis_index("yz")
    y, x = yz // 4, yz % 4
    offsets = sorted(
        [(a, b) for a in range(4) for b in range(4) if (a, b) != (0, 0)],
        key=lambda o: -(min(o[0], 4 - o[0]) + min(o[1], 4 - o[1])),
    )
    peers = [((y + a) % 4) * 4 + (x + b) % 4 for a, b in offsets]
    zs = sorted(range(1, RING), key=lambda o: -min(o, RING - o))
    columns = [(gx + o) % RING for o in zs]
    below, above = (gx + RING - 1) % RING, (gx + 1) % RING
    core = gx % 2
    sibling = gx + 1 - 2 * core

    barrier = pltpu.get_barrier_semaphore()
    for q in peers:
        pl.semaphore_signal(barrier, 1, device_id=(gx, q), device_id_type=MESH)
    for q in columns:
        pl.semaphore_signal(barrier, 1, device_id=(q, yz), device_id_type=MESH)

    loading = [
        pltpu.make_async_copy(linv_hbm, linv, load_sem.at[0]),
        pltpu.make_async_copy(cinv_hbm, cinv, load_sem.at[1]),
        pltpu.make_async_copy(stiff_hbm, stiff, load_sem.at[2]),
    ]
    for copy in loading:
        copy.start()

    sent = []

    def wait_bytes(ref, sem):
        pltpu.make_async_copy(ref, ref, sem).wait()

    def send(src, dst, ssem, rsem, device):
        pltpu.make_async_remote_copy(src, dst, ssem, rsem, device_id=device, device_id_type=MESH).start()

    def to_peers(src, dst, arrivals, ssem, rsem):
        for q in peers:
            send(src(q), dst, ssem, rsem, (gx, q))
        sent.append((arrivals, ssem))

    def to_columns(src, dst, arrivals, ssem, rsem):
        for q in columns:
            send(src, dst, ssem, rsem, (q, yz))
        sent.append((arrivals, ssem))

    lane1 = iota((1, LANES), 1)
    lane8 = iota((8, LANES), 1)
    lane16 = iota((CASES, LANES), 1)
    idx[...] = jnp.full((LANES, LANES), -1, jnp.int32)
    lidx[...] = jnp.full((24, LANES), -1, jnp.int32)
    slot_lane = iota((1, SLOTS), 1)
    for q in range(RING):
        lidx[q : q + 1, 0:SLOTS] = jnp.where(slot_lane < acounts[0:1, q : q + 1], aindex[0, q : q + 1, :], -1)
    idx[0:8, :] = jnp.where(lane8 < 64, lidx[0:8, :], pltpu.roll(lidx[8:16, :], 64, 1))
    face_lane = iota((1, FACE), 1)
    low = jnp.where(face_lane < lcounts[0:1, 0:1], lindex[0, 0:1, :], -1)
    up = jnp.where(face_lane < lcounts[0:1, 1:2], lindex[0, 1:2, :], -1)
    lidx[16:17, 0 : FACE - LANES] = low[:, LANES:FACE]
    lidx[17:18, 0 : FACE - LANES] = up[:, LANES:FACE]
    idx[8:9, :] = low[:, 0:LANES]
    idx[9:10, :] = jnp.where(lane1 < 64, lidx[16:17, :], pltpu.roll(lidx[17:18, :], 64, 1))
    idx[10:11, :] = up[:, 0:LANES]
    lidx[18:19, 0:PRIMAL] = primal[...]
    row_iota = iota((IFACE, LANES), 0)
    for b in range(TILES):
        gather[:, b * LANES : (b + 1) * LANES] = jnp.where(row_iota == idx[b : b + 1, :], 1.0, 0.0).astype(BF16)

    def exchange_values(sends, phase, values):
        out = dot(values, gather[...]).astype(BF16)
        for b in range(TILES):
            sends[phase, b] = out[:, b * LANES : (b + 1) * LANES]

    def exchange_send(phase, sends, arrived, faces, ss, rs, fss, frs):
        to_peers(
            lambda q: sends.at[phase, q % 8], arrived.at[phase, yz], arrived.at[phase, pl.ds(0, 15)],
            ss.at[phase], rs.at[phase],
        )
        send(sends.at[phase, pl.ds(8, 2)], faces.at[phase, 1], fss.at[phase], frs.at[phase], (below, yz))
        send(sends.at[phase, pl.ds(9, 2)], faces.at[phase, 0], fss.at[phase], frs.at[phase], (above, yz))
        sent.append((faces.at[phase], fss.at[phase]))

    def exchange_arrived(phase, arrived, faces, rs, frs):
        wait_bytes(faces.at[phase], frs.at[phase])
        wait_bytes(arrived.at[phase, pl.ds(0, 15)], rs.at[phase])
        lane = iota(arrived.shape[2:], 1)
        first = yz < 8
        mine = (lane < 64) == first
        parts = []
        for b in range(8):
            a, c = arrived[phase, b].astype(F32), arrived[phase, b + 8].astype(F32)
            stay = jnp.where(first, a, c)
            move = jnp.where(first, c, a)
            parts.append(jnp.where(mine, stay, pltpu.roll(move, 64, 1)))
        parts.append(faces[phase, 0, 1].astype(F32))
        tails = jnp.where(lane < 64, faces[phase, 1, 1].astype(F32), faces[phase, 0, 0].astype(F32))
        parts.append(pltpu.roll(tails, 64, 1))
        parts.append(faces[phase, 1, 0].astype(F32))
        return parts

    def exchange_start(phase, values):
        exchange_values(slot_s, phase, values)
        exchange_send(phase, slot_s, slot_r, face_r, slot_ss, slot_rs, face_ss, face_rs)

    def exchange_finish(phase):
        parts = exchange_arrived(phase, slot_r, face_r, slot_rs, face_rs)
        return dot(jnp.concatenate(parts, axis=1).astype(BF16), scatter[...])

    def wide_start(phase, values):
        exchange_values(wide_s, phase, values)
        exchange_send(phase, wide_s, wide_r, wface_r, wide_ss, wide_rs, wface_ss, wface_rs)

    def smooth_start(phase, weighted):
        hi, lo = split(weighted)
        both = dot(jnp.concatenate([hi, lo], axis=0), linv[...])
        part = weight[...] * (both[0:CASES] + both[CASES:])
        hi, lo = split(part)
        wide_start(phase, jnp.concatenate([hi, lo], axis=0))
        return part

    def smooth_finish(phase):
        parts = exchange_arrived(phase, wide_r, wface_r, wide_rs, wface_rs)
        both = dot(jnp.concatenate(parts, axis=1).astype(BF16), scatter[...])
        return both[0:CASES] + both[CASES:]

    def coarse_terms(weighted):
        hi, lo = split(weighted)
        both = dot(jnp.concatenate([hi, lo], axis=0), basis_cols[...])
        return fold(both[0:CASES] + both[CASES:])

    def coarse_start(packed):
        hi, lo = split(packed)
        both = dot(jnp.concatenate([hi, lo], axis=0), spread[...])
        out = (both[0:CASES] + both[CASES:]).astype(BF16)
        half_s[...] = out
        half_r[pl.ds(yz, 1)] = out[None]
        to_peers(lambda q: half_s, half_r.at[yz], half_r.at[pl.ds(0, 15)], one_ss.at[1], one_rs.at[1])

    def coarse_finish():
        wait_bytes(half_r.at[pl.ds(0, 15)], one_rs.at[1])
        total = half_r[0].astype(F32)
        for q in range(1, RING):
            total = total + half_r[q].astype(F32)
        sib_s[...] = total
        send(sib_s, sib_r, one_ss.at[2], one_rs.at[2], (sibling, yz))
        sent.append((sib_s, one_ss.at[2]))
        own = pl.ds(pl.multiple_of(core * HALF, HALF), HALF)
        other = pl.ds(pl.multiple_of((1 - core) * HALF, HALF), HALF)
        picked = dot(total.astype(BF16), near_inverse[own, :])
        rhs[:, own] = total
        wait_bytes(sib_r, one_rs.at[2])
        remote = sib_r[...]
        picked = picked + dot(remote.astype(BF16), near_inverse[other, :])
        rhs[:, other] = remote
        return dot(picked.astype(BF16), near[...])

    def add_up(arrived):
        return sum(arrived[q] for q in range(1, RING)) + arrived[0]

    def parts_start(phase, image):
        hi, lo = split(image)
        both = dot(jnp.concatenate([hi, lo], axis=0), near_t[...])
        hi, lo = split(both[0:CASES] + both[CASES:])
        both = dot(jnp.concatenate([hi, lo], axis=0), chosen_t[...])
        out = both[0:CASES] + both[CASES:]
        for b in range(8):
            for h in range(2):
                part_s[phase, 2 * b + h] = out[8 * h : 8 * h + 8, b * LANES : (b + 1) * LANES]
        part_r[phase, pl.ds(yz, 1)] = part_s[phase, pl.ds(yz, 1)]
        arrivals = part_r.at[phase, pl.ds(0, 15)]
        to_peers(lambda q: part_s.at[phase, q], part_r.at[phase, yz], arrivals, part_ss.at[phase], part_rs.at[phase])

    def sums_start(phase):
        wait_bytes(part_r.at[phase, pl.ds(0, 15)], part_rs.at[phase])
        tile = add_up([part_r[phase, q] for q in range(RING)])
        sum_s[phase] = tile
        sum_r[phase, pl.ds(gx, 1)] = tile[None]
        arrivals = sum_r.at[phase, pl.ds(0, 15)]
        to_columns(sum_s.at[phase], sum_r.at[phase, gx], arrivals, sum_ss.at[phase], sum_rs.at[phase])

    def all_start(phase):
        wait_bytes(sum_r.at[phase, pl.ds(0, 15)], sum_rs.at[phase])
        tile = add_up([sum_r[phase, g] for g in range(RING)])
        all_s[phase] = tile
        all_r[phase, pl.ds(yz, 1)] = tile[None]
        arrivals = all_r.at[phase, pl.ds(0, 15)]
        to_peers(lambda q: all_s.at[phase], all_r.at[phase, yz], arrivals, all_ss.at[phase], all_rs.at[phase])

    def all_finish(phase):
        wait_bytes(all_r.at[phase, pl.ds(0, 15)], all_rs.at[phase])
        tiles = [jnp.concatenate([all_r[phase, 2 * b], all_r[phase, 2 * b + 1]], axis=0) for b in range(8)]
        return jnp.concatenate(tiles, axis=1)

    def coarse_part(values):
        picked = dot(values.astype(BF16), near_inverse[...])
        return dot(picked.astype(BF16), near[...])

    def grams(phase, z, others):
        z_hi, z_lo = split(z)
        highs, lows, at = [], [], 0
        for start, v in others:
            if start > at:
                highs.append(jnp.zeros((start - at, IFACE), BF16))
                lows.append(jnp.zeros((start - at, IFACE), BF16))
            hi, lo = split(v)
            highs.append(hi)
            lows.append(lo)
            at = start + CASES
        highs.append(jnp.zeros((LANES - at, IFACE), BF16))
        lows.append(jnp.zeros((LANES - at, IFACE), BF16))
        one = dot_nt(jnp.concatenate([z_hi, z_lo], axis=0), jnp.concatenate(highs, axis=0))
        two = dot_nt(z_hi, jnp.concatenate(lows, axis=0))
        mine = fold(one[0:CASES] + one[CASES:] + two)
        gram_s[phase] = mine
        gram_r[phase, pl.ds(yz, 1)] = mine[None]
        arrivals = gram_r.at[phase, pl.ds(0, 15)]
        to_peers(lambda q: gram_s.at[phase], gram_r.at[phase, yz], arrivals, gram_ss.at[phase], gram_rs.at[phase])

    def rings_start(phase):
        wait_bytes(gram_r.at[phase, pl.ds(0, 15)], gram_rs.at[phase])
        layer = add_up([gram_r[phase, q] for q in range(RING)])
        ring_s[phase] = layer
        ring_r[phase, pl.ds(gx, 1)] = layer[None]
        arrivals = ring_r.at[phase, pl.ds(0, 15)]
        to_columns(ring_s.at[phase], ring_r.at[phase, gx], arrivals, ring_ss.at[phase], ring_rs.at[phase])

    def rings_finish(phase):
        wait_bytes(ring_r.at[phase, pl.ds(0, 15)], ring_rs.at[phase])
        return unfold(add_up([ring_r[phase, g] for g in range(RING)]))

    for phase in range(3):
        slot_r[phase, pl.ds(yz, 1)] = jnp.zeros((1, CASES, LANES), BF16)
    for phase in range(4):
        wide_r[phase, pl.ds(yz, 1)] = jnp.zeros((1, BLOCK, LANES), BF16)
    prow8 = jnp.broadcast_to(lidx[18:19, :].astype(F32), (8, LANES))
    primals = jnp.where(lane8 < 32, prow8, jnp.where((lane8 >= 64) & (lane8 < 96), pltpu.roll(prow8, 64, 1), 0.0))
    pidx_s[...] = primals
    pidx_rp[pl.ds(yz, 1)] = primals[None]
    pidx_rc[pl.ds(gx, 1)] = primals[None]
    exchange_values(slot_s, 0, loads[...].astype(BF16))

    pl.semaphore_wait(barrier, len(peers) + len(columns))

    exchange_send(0, slot_s, slot_r, face_r, slot_ss, slot_rs, face_ss, face_rs)
    to_columns(pidx_s, pidx_rc.at[gx], pidx_rc.at[pl.ds(0, 15)], one_ss.at[3], one_rs.at[3])
    to_peers(lambda q: pidx_s, pidx_rp.at[yz], pidx_rp.at[pl.ds(0, 15)], one_ss.at[4], one_rs.at[4])
    idx_cols = jnp.transpose(idx[...].astype(F32))
    lane_iota = iota((LANES, IFACE), 1).astype(F32)
    for b in range(TILES):
        scatter[b * LANES : (b + 1) * LANES, :] = jnp.where(idx_cols[:, b : b + 1] == lane_iota, 1.0, 0.0).astype(BF16)
    weight[...] = 1.0 / (1.0 + dot(jnp.ones((CASES, NSLOT), BF16), scatter[...]))
    basis_f32 = basis[...].astype(F32)
    basis_pad = jnp.concatenate([basis_f32, jnp.zeros((LANES - PRIMAL, IFACE), F32)], axis=0)
    basis_cols[...] = jnp.transpose(basis_pad).astype(BF16)
    scaled = jnp.concatenate([weight[...] * basis_pad[0:CASES], weight[...] * basis_pad[CASES:BLOCK]], axis=0)
    scaled = scaled.astype(BF16)
    wide_start(3, scaled)
    loading[0].wait()

    res = loads[...] + exchange_finish(0)
    weighted = weight[...] * res
    mine = coarse_terms(weighted)
    col_s[...] = mine
    col_r[pl.ds(gx, 1)] = mine[None]
    to_columns(col_s, col_r.at[gx], col_r.at[pl.ds(0, 15)], one_ss.at[0], one_rs.at[0])
    own_smooth = smooth_start(0, weighted)
    res_out[...] = res

    wait_bytes(pidx_rc.at[pl.ds(0, 15)], one_rs.at[3])
    owners = jnp.transpose(pack([pidx_rc[g] for g in range(RING)])[0:8])
    half_lane = (iota((PACKED, HALF), 1) + core * HALF).astype(F32)
    spread[...] = jnp.where(owners[:, 0:1] == half_lane, 1.0, 0.0).astype(BF16)

    wait_bytes(pidx_rp.at[pl.ds(0, 15)], one_rs.at[4])
    across_primals = pack([pidx_rp[q] for q in range(RING)])[0:8]
    lower = pidx_rc[pl.ds(below, 1)][0]
    upper = pltpu.roll(pidx_rc[pl.ds(above, 1)][0], 32, 1)
    face_primals = jnp.where(lane8 < 32, lower, jnp.where(lane8 < 64, upper, -1.0))
    near_row = jnp.concatenate([across_primals, face_primals], axis=1)
    chosen = jnp.where(iota((COARSE, EXT), 0).astype(F32) == near_row[0:1], 1.0, 0.0).astype(BF16)
    loading[1].wait()
    near_inverse[...] = dot(cinv[...], chosen).astype(BF16)

    wait_bytes(col_r.at[pl.ds(0, 15)], one_rs.at[0])
    coarse_start(pack([col_r[g] for g in range(RING)]))

    parts = exchange_arrived(3, wide_r, wface_r, wide_rs, wface_rs)
    lane32 = iota((BLOCK, LANES), 1)
    for b in range(8):
        both = jnp.concatenate([jnp.where(lane32 < 64, parts[b], 0.0), jnp.where(lane32 < 64, 0.0, parts[b])], axis=0)
        rows = dot(both.astype(BF16), scatter[b * LANES : (b + 1) * LANES, :]).astype(BF16)
        near[b * BLOCK : (b + 1) * BLOCK, :] = rows[0:BLOCK]
        near[(b + 8) * BLOCK : (b + 9) * BLOCK, :] = rows[BLOCK:]
    none = jnp.zeros((BLOCK, LANES), F32)
    faces = jnp.concatenate([
        jnp.concatenate([parts[8], jnp.where(lane32 < 64, parts[9], 0.0), none], axis=1),
        jnp.concatenate([none, jnp.where(lane32 < 64, 0.0, parts[9]), parts[10]], axis=1),
    ], axis=0)
    near[16 * BLOCK : 18 * BLOCK, :] = dot(faces.astype(BF16), scatter[8 * LANES :, :]).astype(BF16)
    near[18 * BLOCK :, :] = jnp.zeros((EXT - 18 * BLOCK, IFACE), BF16)
    near[pl.ds(pl.multiple_of(yz * BLOCK, BLOCK), BLOCK), :] = scaled
    near_t[...] = jnp.transpose(near[...].astype(F32)).astype(BF16)
    near_col = jnp.transpose(near_row)
    chosen_t[...] = jnp.where(near_col[:, 0:1] == iota((EXT, COARSE), 1).astype(F32), 1.0, 0.0).astype(BF16)

    own_smooth = own_smooth + smooth_finish(0)
    smooth[...] = own_smooth
    loading[2].wait()
    z = own_smooth + coarse_finish()

    image = dot(z.astype(BF16), stiff[...])
    parts_start(0, image)
    grams(0, z, [(32, image), (48, weighted)])
    exchange_start(1, image.astype(BF16))
    sums_start(0)
    rings_start(0)
    image = image + exchange_finish(1)
    own_smooth = smooth_start(1, weight[...] * image)
    img[...] = image
    pre_out[...] = z
    all_start(0)
    first = rings_finish(0)
    alpha = factor_t(eliminate(first, 32), 48)
    res_out[...] = res_out[...] - apply_t(alpha, image)
    sol_out[...] = apply_t(alpha, z)
    own_smooth = own_smooth + smooth_finish(1)
    img_smooth[...] = own_smooth
    own_smooth = smooth[...] - apply_t(alpha, own_smooth)
    smooth[...] = own_smooth
    image_rhs = all_finish(0)
    img_rhs[...] = image_rhs
    coarse = rhs[...] - apply_t(alpha, image_rhs)
    rhs[...] = coarse
    z = own_smooth + coarse_part(coarse)

    image = dot(z.astype(BF16), stiff[...])
    parts_start(1, image)
    grams(1, z, [(0, weight[...] * img[...]), (32, image), (48, weight[...] * res_out[...])])
    exchange_start(2, image.astype(BF16))
    identity = jnp.where(lane16 - 64 == iota((CASES, LANES), 0), 1.0, 0.0)
    inverse = factor_t(eliminate(lanes_of(first, 48) + identity, 48), 64)
    sums_start(1)
    rings_start(1)
    image = image + exchange_finish(2)
    own_smooth = smooth_start(2, weight[...] * image)
    all_start(1)
    second = rings_finish(1)
    cross = jnp.concatenate([jnp.zeros((48, LANES), F32), second, jnp.zeros((64, LANES), F32)], axis=0)
    cross_t = jnp.transpose(cross)[0:CASES, :]
    beta = apply_t(inverse, second)
    beta_t = factor_t(beta, 48)
    curve = apply_t(beta_t, cross_t + apply_t(factor_t(first, 32), beta))
    curve = curve + apply_t(factor_t(cross_t, 48), beta) + pltpu.roll(second, 16, 1)
    system = jnp.where(lane16 < 64, curve, pltpu.roll(second, 16, 1))
    alpha = factor_t(eliminate(system, 48), 64)
    own_smooth = own_smooth + smooth_finish(2) + apply_t(beta_t, img_smooth[...])
    own_smooth = smooth[...] - apply_t(alpha, own_smooth)
    image = image + apply_t(beta_t, img[...])
    res_out[...] = res_out[...] - apply_t(alpha, image)
    direction = z + apply_t(beta_t, pre_out[...])
    sol_out[...] = sol_out[...] + apply_t(alpha, direction)
    image_rhs = all_finish(1) + apply_t(beta_t, img_rhs[...])
    pre_out[...] = own_smooth + coarse_part(rhs[...] - apply_t(alpha, image_rhs))

    for arrivals, ssem in sent:
        wait_bytes(arrivals, ssem)


def hand_over(a, b, c, a_out, b_out, c_out):
    a_out[...] = a[...]
    b_out[...] = b[...]
    c_out[...] = c[...]


def per_device(*args):
    vector = jax.ShapeDtypeStruct((CASES, IFACE), F32)
    vmem = pl.BlockSpec(memory_space=pltpu.VMEM)
    hbm = pl.BlockSpec(memory_space=pl.ANY)
    dma = pltpu.SemaphoreType.DMA
    results = pl.pallas_call(
        kernel,
        out_shape=(vector, vector, vector),
        in_specs=[vmem, hbm, hbm, vmem, hbm, vmem, vmem, vmem, vmem, vmem],
        out_specs=(vmem, vmem, vmem),
        scratch_shapes=[
            pltpu.VMEM((IFACE, IFACE), BF16),
            pltpu.VMEM((IFACE, IFACE), BF16),
            pltpu.VMEM((COARSE, COARSE), BF16),
            pltpu.VMEM((IFACE, NSLOT), BF16),
            pltpu.VMEM((NSLOT, IFACE), BF16),
            pltpu.VMEM((IFACE, LANES), BF16),
            pltpu.VMEM((CASES, IFACE), F32),
            pltpu.VMEM((PACKED, HALF), BF16),
            pltpu.VMEM((EXT, IFACE), BF16),
            pltpu.VMEM((IFACE, EXT), BF16),
            pltpu.VMEM((EXT, COARSE), BF16),
            pltpu.VMEM((COARSE, EXT), BF16),
            pltpu.VMEM((LANES, LANES), jnp.int32),
            pltpu.VMEM((24, LANES), jnp.int32),
            pltpu.VMEM((CASES, IFACE), F32),
            pltpu.VMEM((CASES, COARSE), F32),
            pltpu.VMEM((CASES, IFACE), F32),
            pltpu.VMEM((CASES, IFACE), F32),
            pltpu.VMEM((CASES, COARSE), F32),
            pltpu.VMEM((3, TILES, CASES, LANES), BF16),
            pltpu.VMEM((3, RING, CASES, LANES), BF16),
            pltpu.VMEM((3, 2, 2, CASES, LANES), BF16),
            pltpu.VMEM((4, TILES, BLOCK, LANES), BF16),
            pltpu.VMEM((4, RING, BLOCK, LANES), BF16),
            pltpu.VMEM((4, 2, 2, BLOCK, LANES), BF16),
            pltpu.VMEM((2, 8, LANES), F32),
            pltpu.VMEM((2, RING, 8, LANES), F32),
            pltpu.VMEM((2, 8, LANES), F32),
            pltpu.VMEM((2, RING, 8, LANES), F32),
            pltpu.VMEM((8, LANES), F32),
            pltpu.VMEM((RING, 8, LANES), F32),
            pltpu.VMEM((CASES, HALF), BF16),
            pltpu.VMEM((RING, CASES, HALF), BF16),
            pltpu.VMEM((CASES, HALF), F32),
            pltpu.VMEM((CASES, HALF), F32),
            pltpu.VMEM((2, RING, 8, LANES), F32),
            pltpu.VMEM((2, RING, 8, LANES), F32),
            pltpu.VMEM((2, 8, LANES), F32),
            pltpu.VMEM((2, RING, 8, LANES), F32),
            pltpu.VMEM((2, 8, LANES), F32),
            pltpu.VMEM((2, RING, 8, LANES), F32),
            pltpu.VMEM((8, LANES), F32),
            pltpu.VMEM((RING, 8, LANES), F32),
            pltpu.VMEM((RING, 8, LANES), F32),
            dma((3,)),
            dma((3,)), dma((3,)), dma((3,)), dma((3,)),
            dma((4,)), dma((4,)), dma((4,)), dma((4,)),
            dma((2,)), dma((2,)), dma((2,)), dma((2,)), dma((2,)), dma((2,)), dma((2,)), dma((2,)),
            dma((2,)), dma((2,)), dma((5,)), dma((5,)),
        ],
        compiler_params=pltpu.CompilerParams(
            collective_id=0, has_side_effects=True, vmem_limit_bytes=56 * 2**20
        ),
    )(*args)
    return pl.pallas_call(
        hand_over,
        out_shape=(vector, vector, vector),
        in_specs=[vmem, vmem, vmem],
        out_specs=(vmem, vmem, vmem),
        compiler_params=pltpu.CompilerParams(vmem_limit_bytes=60 * 2**20),
    )(*results)


def solution(mesh):
    whole = ("gx", "yz")
    columns, rows = P(None, whole), P(whole, None)
    lists = P(whole, None, None)
    return jax.shard_map(
        per_device,
        mesh=mesh,
        in_specs=(columns, rows, rows, columns, P(), rows, rows, lists, rows, lists),
        out_specs=(columns, columns, columns),
        check_vma=False,
    )
```

```python
import functools

import jax
import jax.numpy as jnp
from jax import lax
from jax.experimental import pallas as pl
from jax.experimental.pallas import tpu as pltpu
from jax.sharding import PartitionSpec as P

MESH = pl.DeviceIdType.MESH
F32, BF16 = jnp.float32, jnp.bfloat16

CASES = 16
IFACE = 1152
PRIMAL = 24
SLOTS = 48
FACE = 144
COARSE = 1024
RING = 16
TILES = 11
LANES = 128
NSLOT = TILES * LANES
PACKED = 512
HALF = 512
BLOCK = 32
EXT = 640


def dot(a, b):
    return jnp.dot(a, b, preferred_element_type=F32)


def dot_nt(a, b):
    return lax.dot_general(a, b, (((1,), (1,)), ((), ())), preferred_element_type=F32)


def split(x):
    hi = x.astype(BF16)
    return hi, (x - hi.astype(F32)).astype(BF16)


def iota(shape, dim):
    return lax.broadcasted_iota(jnp.int32, shape, dim)


def fold(m):
    lane = iota((8, LANES), 1)
    return jnp.where(lane < 64, m[0:8], pltpu.roll(m[8:16], 64, 1))


def unfold(m):
    return jnp.concatenate([m, pltpu.roll(m, 64, 1)], axis=0)


def pack(tiles):
    lane = iota((8, LANES), 1)
    keep = (lane % 64) < 32
    pairs = []
    for i in range(8):
        even = jnp.where(keep, tiles[2 * i], 0.0)
        odd = jnp.where(keep, tiles[2 * i + 1], 0.0)
        pairs.append(even + pltpu.roll(odd, 32, 1))
    columns = []
    for i in range(4):
        a, b = pairs[2 * i], pairs[2 * i + 1]
        top = jnp.where(lane < 64, a, pltpu.roll(b, 64, 1))
        low = jnp.where(lane < 64, pltpu.roll(a, 64, 1), b)
        columns.append(jnp.concatenate([top, low], axis=0))
    return jnp.concatenate(columns, axis=1)


def eliminate(m, base):
    rows = iota((CASES, LANES), 0)
    for k in range(CASES):
        row = m[k : k + 1, :]
        scaled = row * (1.0 / row[:, base + k : base + k + 1])
        m = jnp.where(rows == k, scaled, m - m[:, base + k : base + k + 1] * scaled)
    return m


def lanes_of(m, start):
    lane = iota(m.shape, 1)
    return jnp.where((lane >= start) & (lane < start + CASES), m, 0.0)


def split3(x):
    a = x.astype(BF16)
    rest = x - a.astype(F32)
    b = rest.astype(BF16)
    return a, b, (rest - b.astype(F32)).astype(BF16)


def factor_t(m, start):
    a, b, c = (part.astype(F32) for part in split3(m))
    stack = jnp.concatenate([a, a, a, b, b, c, jnp.zeros((LANES - 6 * CASES, LANES), F32)], axis=0)
    return jnp.transpose(stack)[start : start + CASES, :].astype(BF16)


def apply_t(left, v):
    a, b, c = split3(v)
    pad = jnp.zeros((LANES - 6 * CASES, v.shape[1]), BF16)
    return dot(left, jnp.concatenate([a, b, c, a, b, a, pad], axis=0))


def kernel(
    loads_hbm, stiff_hbm, linv_hbm, basis_hbm, cinv_hbm, primal_hbm, lcounts_hbm, lindex_hbm, acounts_hbm, aindex_hbm,
    sol_hbm, res_hbm, pre_hbm,
    loads, basis, primal, lcounts, lindex, acounts, aindex, sol_out, res_out, pre_out,
    stiff, linv, cinv, gather, scatter, basis_cols, weight, spread, near, to_coarse, from_coarse, near_inverse,
    idx, lidx, smooth, rhs, img, img_smooth, img_rhs,
    slot_s, slot_r, face_r, wide_s, wide_r, wface_r, gram_s, gram_r, ring_s, ring_r, col_s, col_r,
    half_s, half_r, sib_s, sib_r, part_s, part_r, sum_s, sum_r, all_s, all_r, pidx_s, pidx_rp, pidx_rc,
    load_sem, store_sem, slot_ss, slot_rs, face_ss, face_rs, wide_ss, wide_rs, wface_ss, wface_rs,
    gram_ss, gram_rs, ring_ss, ring_rs, part_ss, part_rs, sum_ss, sum_rs, all_ss, all_rs, one_ss, one_rs,
):
    gx, yz = lax.axis_index("gx"), lax.axis_index("yz")
    y, x = yz // 4, yz % 4
    offsets = sorted(
        [(a, b) for a in range(4) for b in range(4) if (a, b) != (0, 0)],
        key=lambda o: -(min(o[0], 4 - o[0]) + min(o[1], 4 - o[1])),
    )
    peers = [((y + a) % 4) * 4 + (x + b) % 4 for a, b in offsets]
    zs = sorted(range(1, RING), key=lambda o: -min(o, RING - o))
    columns = [(gx + o) % RING for o in zs]
    below, above = (gx + RING - 1) % RING, (gx + 1) % RING
    core = gx % 2
    sibling = gx + 1 - 2 * core

    barrier = pltpu.get_barrier_semaphore()
    for q in peers:
        pl.semaphore_signal(barrier, 1, device_id=(gx, q), device_id_type=MESH)
    for q in columns:
        pl.semaphore_signal(barrier, 1, device_id=(q, yz), device_id_type=MESH)

    lists = [(primal_hbm, primal), (lcounts_hbm, lcounts), (lindex_hbm, lindex), (acounts_hbm, acounts), (aindex_hbm, aindex)]
    order = [*lists, (loads_hbm, loads), (basis_hbm, basis), (linv_hbm, linv), (cinv_hbm, cinv), (stiff_hbm, stiff)]
    loading = [pltpu.make_async_copy(src, dst, load_sem.at[i]) for i, (src, dst) in enumerate(order)]
    for copy in loading:
        copy.start()

    sent = []

    def wait_bytes(ref, sem):
        pltpu.make_async_copy(ref, ref, sem).wait()

    def send(src, dst, ssem, rsem, device):
        pltpu.make_async_remote_copy(src, dst, ssem, rsem, device_id=device, device_id_type=MESH).start()

    def to_peers(src, dst, arrivals, ssem, rsem):
        for q in peers:
            send(src(q), dst, ssem, rsem, (gx, q))
        sent.append((arrivals, ssem))

    def to_columns(src, dst, arrivals, ssem, rsem):
        for q in columns:
            send(src, dst, ssem, rsem, (q, yz))
        sent.append((arrivals, ssem))

    lane1 = iota((1, LANES), 1)
    lane8 = iota((8, LANES), 1)
    lane16 = iota((CASES, LANES), 1)
    idx[...] = jnp.full((LANES, LANES), -1, jnp.int32)
    lidx[...] = jnp.full((24, LANES), -1, jnp.int32)
    for copy in loading[0:5]:
        copy.wait()
    slot_lane = iota((1, SLOTS), 1)
    for q in range(RING):
        lidx[q : q + 1, 0:SLOTS] = jnp.where(slot_lane < acounts[0:1, q : q + 1], aindex[0, q : q + 1, :], -1)
    idx[0:8, :] = jnp.where(lane8 < 64, lidx[0:8, :], pltpu.roll(lidx[8:16, :], 64, 1))
    face_lane = iota((1, FACE), 1)
    low = jnp.where(face_lane < lcounts[0:1, 0:1], lindex[0, 0:1, :], -1)
    up = jnp.where(face_lane < lcounts[0:1, 1:2], lindex[0, 1:2, :], -1)
    lidx[16:17, 0 : FACE - LANES] = low[:, LANES:FACE]
    lidx[17:18, 0 : FACE - LANES] = up[:, LANES:FACE]
    idx[8:9, :] = low[:, 0:LANES]
    idx[9:10, :] = jnp.where(lane1 < 64, lidx[16:17, :], pltpu.roll(lidx[17:18, :], 64, 1))
    idx[10:11, :] = up[:, 0:LANES]
    lidx[18:19, 0:PRIMAL] = primal[...]
    row_iota = iota((IFACE, LANES), 0)
    for b in range(TILES):
        gather[:, b * LANES : (b + 1) * LANES] = jnp.where(row_iota == idx[b : b + 1, :], 1.0, 0.0).astype(BF16)

    def exchange_values(sends, phase, values):
        out = dot(values, gather[...]).astype(BF16)
        for b in range(TILES):
            sends[phase, b] = out[:, b * LANES : (b + 1) * LANES]

    def exchange_send(phase, sends, arrived, faces, ss, rs, fss, frs):
        to_peers(
            lambda q: sends.at[phase, q % 8], arrived.at[phase, yz], arrived.at[phase, pl.ds(0, 15)],
            ss.at[phase], rs.at[phase],
        )
        send(sends.at[phase, pl.ds(8, 2)], faces.at[phase, 1], fss.at[phase], frs.at[phase], (below, yz))
        send(sends.at[phase, pl.ds(9, 2)], faces.at[phase, 0], fss.at[phase], frs.at[phase], (above, yz))
        sent.append((faces.at[phase], fss.at[phase]))

    def exchange_arrived(phase, arrived, faces, rs, frs):
        wait_bytes(faces.at[phase], frs.at[phase])
        wait_bytes(arrived.at[phase, pl.ds(0, 15)], rs.at[phase])
        lane = iota(arrived.shape[2:], 1)
        first = yz < 8
        mine = (lane < 64) == first
        parts = []
        for b in range(8):
            a, c = arrived[phase, b].astype(F32), arrived[phase, b + 8].astype(F32)
            stay = jnp.where(first, a, c)
            move = jnp.where(first, c, a)
            parts.append(jnp.where(mine, stay, pltpu.roll(move, 64, 1)))
        parts.append(faces[phase, 0, 1].astype(F32))
        tails = jnp.where(lane < 64, faces[phase, 1, 1].astype(F32), faces[phase, 0, 0].astype(F32))
        parts.append(pltpu.roll(tails, 64, 1))
        parts.append(faces[phase, 1, 0].astype(F32))
        return parts

    def exchange_start(phase, values):
        exchange_values(slot_s, phase, values)
        exchange_send(phase, slot_s, slot_r, face_r, slot_ss, slot_rs, face_ss, face_rs)

    def exchange_finish(phase):
        parts = exchange_arrived(phase, slot_r, face_r, slot_rs, face_rs)
        return dot(jnp.concatenate(parts, axis=1).astype(BF16), scatter[...])

    def wide_start(phase, values):
        exchange_values(wide_s, phase, values)
        exchange_send(phase, wide_s, wide_r, wface_r, wide_ss, wide_rs, wface_ss, wface_rs)

    def smooth_start(phase, weighted):
        hi, lo = split(weighted)
        both = dot(jnp.concatenate([hi, lo], axis=0), linv[...])
        part = weight[...] * (both[0:CASES] + both[CASES:])
        hi, lo = split(part)
        wide_start(phase, jnp.concatenate([hi, lo], axis=0))
        return part

    def smooth_finish(phase):
        parts = exchange_arrived(phase, wide_r, wface_r, wide_rs, wface_rs)
        both = dot(jnp.concatenate(parts, axis=1).astype(BF16), scatter[...])
        return both[0:CASES] + both[CASES:]

    def coarse_terms(weighted):
        hi, lo = split(weighted)
        both = dot(jnp.concatenate([hi, lo], axis=0), basis_cols[...])
        return fold(both[0:CASES] + both[CASES:])

    def coarse_start(packed):
        hi, lo = split(packed)
        both = dot(jnp.concatenate([hi, lo], axis=0), spread[...])
        out = (both[0:CASES] + both[CASES:]).astype(BF16)
        half_s[...] = out
        half_r[pl.ds(yz, 1)] = out[None]
        to_peers(lambda q: half_s, half_r.at[yz], half_r.at[pl.ds(0, 15)], one_ss.at[1], one_rs.at[1])

    def coarse_finish():
        wait_bytes(half_r.at[pl.ds(0, 15)], one_rs.at[1])
        total = half_r[0].astype(F32)
        for q in range(1, RING):
            total = total + half_r[q].astype(F32)
        sib_s[...] = total
        send(sib_s, sib_r, one_ss.at[2], one_rs.at[2], (sibling, yz))
        sent.append((sib_s, one_ss.at[2]))
        own = pl.ds(pl.multiple_of(core * HALF, HALF), HALF)
        other = pl.ds(pl.multiple_of((1 - core) * HALF, HALF), HALF)
        picked = dot(total.astype(BF16), near_inverse[own, :])
        rhs[:, own] = total
        wait_bytes(sib_r, one_rs.at[2])
        remote = sib_r[...]
        picked = picked + dot(remote.astype(BF16), near_inverse[other, :])
        rhs[:, other] = remote
        return dot(picked.astype(BF16), near[...])

    def add_up(arrived):
        return sum(arrived[q] for q in range(1, RING)) + arrived[0]

    def parts_start(phase, image):
        hi, lo = split(image)
        both = dot(jnp.concatenate([hi, lo], axis=0), to_coarse[...])
        out = both[0:CASES] + both[CASES:]
        for b in range(8):
            for h in range(2):
                part_s[phase, 2 * b + h] = out[8 * h : 8 * h + 8, b * LANES : (b + 1) * LANES]
        part_r[phase, pl.ds(yz, 1)] = part_s[phase, pl.ds(yz, 1)]
        arrivals = part_r.at[phase, pl.ds(0, 15)]
        to_peers(lambda q: part_s.at[phase, q], part_r.at[phase, yz], arrivals, part_ss.at[phase], part_rs.at[phase])

    def sums_start(phase):
        wait_bytes(part_r.at[phase, pl.ds(0, 15)], part_rs.at[phase])
        tile = add_up([part_r[phase, q] for q in range(RING)])
        sum_s[phase] = tile
        sum_r[phase, pl.ds(gx, 1)] = tile[None]
        arrivals = sum_r.at[phase, pl.ds(0, 15)]
        to_columns(sum_s.at[phase], sum_r.at[phase, gx], arrivals, sum_ss.at[phase], sum_rs.at[phase])

    def all_start(phase):
        wait_bytes(sum_r.at[phase, pl.ds(0, 15)], sum_rs.at[phase])
        tile = add_up([sum_r[phase, g] for g in range(RING)])
        all_s[phase] = tile
        all_r[phase, pl.ds(yz, 1)] = tile[None]
        arrivals = all_r.at[phase, pl.ds(0, 15)]
        to_peers(lambda q: all_s.at[phase], all_r.at[phase, yz], arrivals, all_ss.at[phase], all_rs.at[phase])

    def all_finish(phase):
        wait_bytes(all_r.at[phase, pl.ds(0, 15)], all_rs.at[phase])
        tiles = [jnp.concatenate([all_r[phase, 2 * b], all_r[phase, 2 * b + 1]], axis=0) for b in range(8)]
        return jnp.concatenate(tiles, axis=1)

    def coarse_part(values):
        return dot(values.astype(BF16), from_coarse[...])

    def grams(phase, z, others):
        z_hi, z_lo = split(z)
        highs, lows, at = [], [], 0
        for start, v in others:
            if start > at:
                highs.append(jnp.zeros((start - at, IFACE), BF16))
                lows.append(jnp.zeros((start - at, IFACE), BF16))
            hi, lo = split(v)
            highs.append(hi)
            lows.append(lo)
            at = start + CASES
        highs.append(jnp.zeros((LANES - at, IFACE), BF16))
        lows.append(jnp.zeros((LANES - at, IFACE), BF16))
        one = dot_nt(jnp.concatenate([z_hi, z_lo], axis=0), jnp.concatenate(highs, axis=0))
        two = dot_nt(z_hi, jnp.concatenate(lows, axis=0))
        mine = fold(one[0:CASES] + one[CASES:] + two)
        gram_s[phase] = mine
        gram_r[phase, pl.ds(yz, 1)] = mine[None]
        arrivals = gram_r.at[phase, pl.ds(0, 15)]
        to_peers(lambda q: gram_s.at[phase], gram_r.at[phase, yz], arrivals, gram_ss.at[phase], gram_rs.at[phase])

    def rings_start(phase):
        wait_bytes(gram_r.at[phase, pl.ds(0, 15)], gram_rs.at[phase])
        layer = add_up([gram_r[phase, q] for q in range(RING)])
        ring_s[phase] = layer
        ring_r[phase, pl.ds(gx, 1)] = layer[None]
        arrivals = ring_r.at[phase, pl.ds(0, 15)]
        to_columns(ring_s.at[phase], ring_r.at[phase, gx], arrivals, ring_ss.at[phase], ring_rs.at[phase])

    def rings_finish(phase):
        wait_bytes(ring_r.at[phase, pl.ds(0, 15)], ring_rs.at[phase])
        return unfold(add_up([ring_r[phase, g] for g in range(RING)]))

    for phase in range(3):
        slot_r[phase, pl.ds(yz, 1)] = jnp.zeros((1, CASES, LANES), BF16)
    for phase in range(4):
        wide_r[phase, pl.ds(yz, 1)] = jnp.zeros((1, BLOCK, LANES), BF16)
    prow8 = jnp.broadcast_to(lidx[18:19, :].astype(F32), (8, LANES))
    primals = jnp.where(lane8 < 32, prow8, jnp.where((lane8 >= 64) & (lane8 < 96), pltpu.roll(prow8, 64, 1), 0.0))
    pidx_s[...] = primals
    pidx_rp[pl.ds(yz, 1)] = primals[None]
    pidx_rc[pl.ds(gx, 1)] = primals[None]
    loading[5].wait()
    exchange_values(slot_s, 0, loads[...].astype(BF16))

    pl.semaphore_wait(barrier, len(peers) + len(columns))

    exchange_send(0, slot_s, slot_r, face_r, slot_ss, slot_rs, face_ss, face_rs)
    to_columns(pidx_s, pidx_rc.at[gx], pidx_rc.at[pl.ds(0, 15)], one_ss.at[3], one_rs.at[3])
    to_peers(lambda q: pidx_s, pidx_rp.at[yz], pidx_rp.at[pl.ds(0, 15)], one_ss.at[4], one_rs.at[4])
    idx_cols = jnp.transpose(idx[...].astype(F32))
    lane_iota = iota((LANES, IFACE), 1).astype(F32)
    for b in range(TILES):
        scatter[b * LANES : (b + 1) * LANES, :] = jnp.where(idx_cols[:, b : b + 1] == lane_iota, 1.0, 0.0).astype(BF16)
    weight[...] = 1.0 / (1.0 + dot(jnp.ones((CASES, NSLOT), BF16), scatter[...]))
    loading[6].wait()
    basis_f32 = basis[...].astype(F32)
    basis_pad = jnp.concatenate([basis_f32, jnp.zeros((LANES - PRIMAL, IFACE), F32)], axis=0)
    basis_cols[...] = jnp.transpose(basis_pad).astype(BF16)
    scaled = jnp.concatenate([weight[...] * basis_pad[0:CASES], weight[...] * basis_pad[CASES:BLOCK]], axis=0)
    scaled = scaled.astype(BF16)
    wide_start(3, scaled)
    loading[7].wait()

    res = loads[...] + exchange_finish(0)
    weighted = weight[...] * res
    mine = coarse_terms(weighted)
    col_s[...] = mine
    col_r[pl.ds(gx, 1)] = mine[None]
    to_columns(col_s, col_r.at[gx], col_r.at[pl.ds(0, 15)], one_ss.at[0], one_rs.at[0])
    own_smooth = smooth_start(0, weighted)
    res_out[...] = res

    wait_bytes(pidx_rc.at[pl.ds(0, 15)], one_rs.at[3])
    owners = jnp.transpose(pack([pidx_rc[g] for g in range(RING)])[0:8])
    half_lane = (iota((PACKED, HALF), 1) + core * HALF).astype(F32)
    spread[...] = jnp.where(owners[:, 0:1] == half_lane, 1.0, 0.0).astype(BF16)

    wait_bytes(pidx_rp.at[pl.ds(0, 15)], one_rs.at[4])
    across_primals = pack([pidx_rp[q] for q in range(RING)])[0:8]
    lower = pidx_rc[pl.ds(below, 1)][0]
    upper = pltpu.roll(pidx_rc[pl.ds(above, 1)][0], 32, 1)
    face_primals = jnp.where(lane8 < 32, lower, jnp.where(lane8 < 64, upper, -1.0))
    near_row = jnp.concatenate([across_primals, face_primals], axis=1)
    chosen = jnp.where(iota((COARSE, EXT), 0).astype(F32) == near_row[0:1], 1.0, 0.0).astype(BF16)
    loading[8].wait()
    near_inverse[...] = dot(cinv[...], chosen).astype(BF16)

    wait_bytes(col_r.at[pl.ds(0, 15)], one_rs.at[0])
    coarse_start(pack([col_r[g] for g in range(RING)]))

    parts = exchange_arrived(3, wide_r, wface_r, wide_rs, wface_rs)
    lane32 = iota((BLOCK, LANES), 1)
    for b in range(8):
        both = jnp.concatenate([jnp.where(lane32 < 64, parts[b], 0.0), jnp.where(lane32 < 64, 0.0, parts[b])], axis=0)
        rows = dot(both.astype(BF16), scatter[b * LANES : (b + 1) * LANES, :]).astype(BF16)
        near[b * BLOCK : (b + 1) * BLOCK, :] = rows[0:BLOCK]
        near[(b + 8) * BLOCK : (b + 9) * BLOCK, :] = rows[BLOCK:]
    none = jnp.zeros((BLOCK, LANES), F32)
    faces = jnp.concatenate([
        jnp.concatenate([parts[8], jnp.where(lane32 < 64, parts[9], 0.0), none], axis=1),
        jnp.concatenate([none, jnp.where(lane32 < 64, 0.0, parts[9]), parts[10]], axis=1),
    ], axis=0)
    near[16 * BLOCK : 18 * BLOCK, :] = dot(faces.astype(BF16), scatter[8 * LANES :, :]).astype(BF16)
    near[18 * BLOCK :, :] = jnp.zeros((EXT - 18 * BLOCK, IFACE), BF16)
    near[pl.ds(pl.multiple_of(yz * BLOCK, BLOCK), BLOCK), :] = scaled
    near_t = jnp.transpose(near[...].astype(F32)).astype(BF16)
    near_col = jnp.transpose(near_row)
    chosen_t = jnp.where(near_col[:, 0:1] == iota((EXT, COARSE), 1).astype(F32), 1.0, 0.0).astype(BF16)
    to_coarse[...] = dot(near_t, chosen_t).astype(BF16)

    own_smooth = own_smooth + smooth_finish(0)
    smooth[...] = own_smooth
    loading[9].wait()
    z = own_smooth + coarse_finish()

    image = dot(z.astype(BF16), stiff[...])
    parts_start(0, image)
    grams(0, z, [(32, image), (48, weighted)])
    exchange_start(1, image.astype(BF16))
    from_coarse[...] = dot(near_inverse[...], near[...]).astype(BF16)
    sums_start(0)
    rings_start(0)
    image = image + exchange_finish(1)
    own_smooth = smooth_start(1, weight[...] * image)
    img[...] = image
    pre_out[...] = z
    all_start(0)
    first = rings_finish(0)
    alpha = factor_t(eliminate(first, 32), 48)
    res_out[...] = res_out[...] - apply_t(alpha, image)
    sol_out[...] = apply_t(alpha, z)
    own_smooth = own_smooth + smooth_finish(1)
    img_smooth[...] = own_smooth
    own_smooth = smooth[...] - apply_t(alpha, own_smooth)
    smooth[...] = own_smooth
    image_rhs = all_finish(0)
    img_rhs[...] = image_rhs
    coarse = rhs[...] - apply_t(alpha, image_rhs)
    rhs[...] = coarse
    z = own_smooth + coarse_part(coarse)

    image = dot(z.astype(BF16), stiff[...])
    parts_start(1, image)
    grams(1, z, [(0, weight[...] * img[...]), (32, image), (48, weight[...] * res_out[...])])
    exchange_start(2, image.astype(BF16))
    identity = jnp.where(lane16 - 64 == iota((CASES, LANES), 0), 1.0, 0.0)
    inverse = factor_t(eliminate(lanes_of(first, 48) + identity, 48), 64)
    sums_start(1)
    rings_start(1)
    image = image + exchange_finish(2)
    own_smooth = smooth_start(2, weight[...] * image)
    all_start(1)
    second = rings_finish(1)
    cross = jnp.concatenate([jnp.zeros((48, LANES), F32), second, jnp.zeros((64, LANES), F32)], axis=0)
    cross_t = jnp.transpose(cross)[0:CASES, :]
    beta = apply_t(inverse, second)
    beta_t = factor_t(beta, 48)
    curve = apply_t(beta_t, cross_t + apply_t(factor_t(first, 32), beta))
    curve = curve + apply_t(factor_t(cross_t, 48), beta) + pltpu.roll(second, 16, 1)
    system = jnp.where(lane16 < 64, curve, pltpu.roll(second, 16, 1))
    alpha = factor_t(eliminate(system, 48), 64)
    own_smooth = own_smooth + smooth_finish(2) + apply_t(beta_t, img_smooth[...])
    own_smooth = smooth[...] - apply_t(alpha, own_smooth)
    image = image + apply_t(beta_t, img[...])
    res_out[...] = res_out[...] - apply_t(alpha, image)
    direction = z + apply_t(beta_t, pre_out[...])
    sol_out[...] = sol_out[...] + apply_t(alpha, direction)
    image_rhs = all_finish(1) + apply_t(beta_t, img_rhs[...])
    results = [(sol_out, sol_hbm), (res_out, res_hbm), (pre_out, pre_hbm)]
    storing = [pltpu.make_async_copy(src, dst, store_sem.at[i]) for i, (src, dst) in enumerate(results)]
    storing[0].start()
    storing[1].start()
    pre_out[...] = own_smooth + coarse_part(rhs[...] - apply_t(alpha, image_rhs))

    storing[2].start()
    for arrivals, ssem in sent:
        wait_bytes(arrivals, ssem)
    for copy in storing:
        copy.wait()


def hand_over(a, b, c, a_out, b_out, c_out):
    a_out[...] = a[...]
    b_out[...] = b[...]
    c_out[...] = c[...]


def per_device(*args):
    vector = jax.ShapeDtypeStruct((CASES, IFACE), F32)
    hbm = pl.BlockSpec(memory_space=pl.ANY)
    dma = pltpu.SemaphoreType.DMA
    results = pl.pallas_call(
        kernel,
        out_shape=(vector, vector, vector),
        in_specs=[hbm] * 10,
        out_specs=(hbm, hbm, hbm),
        scratch_shapes=[
            pltpu.VMEM((CASES, IFACE), F32),
            pltpu.VMEM((PRIMAL, IFACE), BF16),
            pltpu.VMEM((1, PRIMAL), jnp.int32),
            pltpu.VMEM((1, 2), jnp.int32),
            pltpu.VMEM((1, 2, FACE), jnp.int32),
            pltpu.VMEM((1, RING), jnp.int32),
            pltpu.VMEM((1, RING, SLOTS), jnp.int32),
            pltpu.VMEM((CASES, IFACE), F32),
            pltpu.VMEM((CASES, IFACE), F32),
            pltpu.VMEM((CASES, IFACE), F32),
            pltpu.VMEM((IFACE, IFACE), BF16),
            pltpu.VMEM((IFACE, IFACE), BF16),
            pltpu.VMEM((COARSE, COARSE), BF16),
            pltpu.VMEM((IFACE, NSLOT), BF16),
            pltpu.VMEM((NSLOT, IFACE), BF16),
            pltpu.VMEM((IFACE, LANES), BF16),
            pltpu.VMEM((CASES, IFACE), F32),
            pltpu.VMEM((PACKED, HALF), BF16),
            pltpu.VMEM((EXT, IFACE), BF16),
            pltpu.VMEM((IFACE, COARSE), BF16),
            pltpu.VMEM((COARSE, IFACE), BF16),
            pltpu.VMEM((COARSE, EXT), BF16),
            pltpu.VMEM((LANES, LANES), jnp.int32),
            pltpu.VMEM((24, LANES), jnp.int32),
            pltpu.VMEM((CASES, IFACE), F32),
            pltpu.VMEM((CASES, COARSE), F32),
            pltpu.VMEM((CASES, IFACE), F32),
            pltpu.VMEM((CASES, IFACE), F32),
            pltpu.VMEM((CASES, COARSE), F32),
            pltpu.VMEM((3, TILES, CASES, LANES), BF16),
            pltpu.VMEM((3, RING, CASES, LANES), BF16),
            pltpu.VMEM((3, 2, 2, CASES, LANES), BF16),
            pltpu.VMEM((4, TILES, BLOCK, LANES), BF16),
            pltpu.VMEM((4, RING, BLOCK, LANES), BF16),
            pltpu.VMEM((4, 2, 2, BLOCK, LANES), BF16),
            pltpu.VMEM((2, 8, LANES), F32),
            pltpu.VMEM((2, RING, 8, LANES), F32),
            pltpu.VMEM((2, 8, LANES), F32),
            pltpu.VMEM((2, RING, 8, LANES), F32),
            pltpu.VMEM((8, LANES), F32),
            pltpu.VMEM((RING, 8, LANES), F32),
            pltpu.VMEM((CASES, HALF), BF16),
            pltpu.VMEM((RING, CASES, HALF), BF16),
            pltpu.VMEM((CASES, HALF), F32),
            pltpu.VMEM((CASES, HALF), F32),
            pltpu.VMEM((2, RING, 8, LANES), F32),
            pltpu.VMEM((2, RING, 8, LANES), F32),
            pltpu.VMEM((2, 8, LANES), F32),
            pltpu.VMEM((2, RING, 8, LANES), F32),
            pltpu.VMEM((2, 8, LANES), F32),
            pltpu.VMEM((2, RING, 8, LANES), F32),
            pltpu.VMEM((8, LANES), F32),
            pltpu.VMEM((RING, 8, LANES), F32),
            pltpu.VMEM((RING, 8, LANES), F32),
            dma((10,)), dma((3,)),
            dma((3,)), dma((3,)), dma((3,)), dma((3,)),
            dma((4,)), dma((4,)), dma((4,)), dma((4,)),
            dma((2,)), dma((2,)), dma((2,)), dma((2,)), dma((2,)), dma((2,)), dma((2,)), dma((2,)),
            dma((2,)), dma((2,)), dma((5,)), dma((5,)),
        ],
        compiler_params=pltpu.CompilerParams(
            collective_id=0, has_side_effects=True, vmem_limit_bytes=56 * 2**20
        ),
    )(*args)
    vmem = pl.BlockSpec(memory_space=pltpu.VMEM)
    return pl.pallas_call(
        hand_over,
        out_shape=(vector, vector, vector),
        in_specs=[vmem, vmem, vmem],
        out_specs=(vmem, vmem, vmem),
        compiler_params=pltpu.CompilerParams(vmem_limit_bytes=60 * 2**20),
    )(*results)


def solution(mesh):
    whole = ("gx", "yz")
    columns, rows = P(None, whole), P(whole, None)
    lists = P(whole, None, None)
    return jax.shard_map(
        per_device,
        mesh=mesh,
        in_specs=(columns, rows, rows, columns, P(), rows, rows, lists, rows, lists),
        out_specs=(columns, columns, columns),
        check_vma=False,
    )
```
